256 devices in a mesh: row: 8 (over y_lo, x), col: 32 (over y_hi, z, core).
Axes of the slice: x: 4, y: 4 (y_hi: 2, y_lo: 2; y = y_hi * 2 + y_lo), z: 8, core: 2. Of those that a mesh axis runs over, the one named last changes fastest.
Arguments:
- tokens: float32 [128, 512, 256], P('row', 'col'), may hold values from -6 to 6
- region_ids: int32 [128, 512], P('row', 'col'), may hold values from 0 to 15, as said below
- bias_index: int32 [256, 256], replicated, may hold values from 0 to 960
- norm_gain: float32 [2, 2, 256], replicated, may hold values from 0.1 to 1.9
- norm_shift: float32 [2, 2, 256], replicated, may hold values from -3 to 3
- qkv_weight: bfloat16 [2, 256, 768], replicated
- proj_weight: bfloat16 [2, 256, 256], replicated, may hold values from -0.375 to 0.375
- expand_weight: bfloat16 [2, 256, 1024], replicated, may hold values from -0.375 to 0.375
- reduce_weight: bfloat16 [2, 1024, 256], replicated, may hold values from -0.1875 to 0.1875
- bias_table: float32 [2, 8, 961], replicated, may hold values from -4 to 4
Outputs:
- mixed_map: float32 [128, 512, 256], P('row', 'col')
The draws below stay inside these ranges and needn't reach their ends.
Inputs may be any that keep to these rules, and one draw needn't show every extreme that they name: `region_ids`: the map is cut into rectangles by three row cuts and three column cuts; a position's label is 4 times its row band plus its column band.
All inputs are finite; a program needn't handle non-finite values.
Results may differ from the reference program's by a relative error of at most 0.019.
Values sent between devices are 32-bit elements; how exact they have to be, the bound alone decides.
No kernel may reach another device: no remote copies, remote signals or barrier semaphores. Data moves between devices by JAX's collectives and lax.ppermute only.
A program may use at most 128 MiB of HBM per device.

```python
import math
import jax
import jax.numpy as jnp
from jax import lax

C = 256
HEADS = 8
HID = 1024
WIN = 16
SHIFT = 8
BIAS_ROWS = 961
NH = 128
NW = 512


def draw_region_ids(key, part):
    key = jax.random.fold_in(key, 23)
    row_key, col_key = jax.random.split(key)
    row_cuts = jax.random.randint(row_key, (3,), 1, NH)
    col_cuts = jax.random.randint(col_key, (3,), 1, NW)
    row_band = jnp.sum((jnp.arange(NH)[:, None] >= row_cuts[None, :]).astype(jnp.int32), 1)
    col_band = jnp.sum((jnp.arange(NW)[:, None] >= col_cuts[None, :]).astype(jnp.int32), 1)
    return (row_band[:, None] * 4 + col_band[None, :]).astype(jnp.int32)


def draw_qkv_weight(key, part):
    key = jax.random.fold_in(key, 11)
    weight = jax.random.normal(key, (2, C, 3 * C), jnp.float32) / math.sqrt(C)
    return weight.astype(jnp.bfloat16)


def place_ends(values, rng, low, largest):
    longest = values.shape.index(max(values.shape))
    spots = []
    for shift in (0, 1):
        where = [jax.random.randint(jax.random.fold_in(rng, axis), (), 0, length) for axis, length in enumerate(values.shape)]
        where[longest] = (where[longest] + shift) % values.shape[longest]
        spots.append(tuple(where))
    return values.at[spots[0]].set(low).at[spots[1]].set(largest)


def shard_levels(own_key, dims, pieces, least, high):
    level = 1.0
    for position, shards_of in pieces:
        steps = jax.random.uniform(jax.random.fold_in(jax.random.fold_in(own_key, 6), position), (shards_of,), jnp.float32, least / len(pieces), high / len(pieces))
        level = level * jnp.repeat(jnp.exp(steps), dims[position] // shards_of).reshape((-1,) + (1,) * (len(dims) - 1 - position))
    return level


def scatter_about(key, shape, width, reach, cuts=(), kind=jnp.bfloat16):
    values = jax.random.normal(key, shape, jnp.float32) * width
    if len(cuts) > 0:
        values = shard_levels(key, shape, cuts, -0.22, 0.18) * values
    return jnp.clip(values, min=-reach, max=reach).astype(kind)


def setup_inputs(seed: int = 0) -> dict:
    key_of = jax.random.split(jax.random.key(seed), 11)
    tokens = scatter_about(key_of[0], (NH, NW, C), 1.0, 6.0, ((0, 8), (1, 32)), jnp.float32)
    region_ids = draw_region_ids(jax.random.fold_in(key_of[10], 71), 0)
    bias_index = place_ends(jax.random.randint(key_of[2], (WIN * WIN, WIN * WIN), 0, BIAS_ROWS), jax.random.fold_in(key_of[2], 1), 0, BIAS_ROWS - 1).astype(jnp.int32)
    norm_gain = jnp.clip(1.0 + 0.18 * jax.random.normal(key_of[3], (2, 2, C), jnp.float32), 0.1, 1.9)
    norm_shift = scatter_about(key_of[4], (2, 2, C), 0.5, 3.0, (), jnp.float32)
    qkv_weight = draw_qkv_weight(jax.random.fold_in(key_of[10], 71), 0)
    proj_weight = scatter_about(key_of[6], (2, C, C), C ** -0.5, 0.375)
    expand_weight = scatter_about(key_of[7], (2, C, HID), C ** -0.5, 0.375)
    reduce_weight = scatter_about(key_of[8], (2, HID, C), HID ** -0.5, 0.1875)
    bias_table = scatter_about(key_of[9], (2, HEADS, BIAS_ROWS), 1.0, 4.0, (), jnp.float32)
    return {"tokens": tokens, "region_ids": region_ids, "bias_index": bias_index, "norm_gain": norm_gain, "norm_shift": norm_shift, "qkv_weight": qkv_weight, "proj_weight": proj_weight, "expand_weight": expand_weight, "reduce_weight": reduce_weight, "bias_table": bias_table}


def layer_norm(tile, gain, offset):
    center = tile - lax.optimization_barrier(jnp.mean(tile, -1, keepdims=True))
    spread = lax.optimization_barrier(jnp.mean(center * center, -1, keepdims=True))
    return (center * lax.rsqrt(spread + 1e-05) * gain + offset).astype(jnp.bfloat16)

def to_windows(array, tile_rows, tile_cols):
    trailing = array.shape[2:]
    array = array.reshape((tile_rows // WIN, WIN, tile_cols // WIN, WIN) + trailing)
    permuted = (0, 2, 1, 3) + tuple(range(4, 4 + len(trailing)))
    return jnp.transpose(array, permuted).reshape((-1, WIN * WIN) + trailing)

def from_windows(array, tile_rows, tile_cols):
    trailing = array.shape[2:]
    array = array.reshape((tile_rows // WIN, tile_cols // WIN, WIN, WIN) + trailing)
    permuted = (0, 2, 1, 3) + tuple(range(4, 4 + len(trailing)))
    return jnp.transpose(array, permuted).reshape((tile_rows, tile_cols) + trailing)

def swin_block(tile, layer, region, bias_index, norm_gain, norm_shift, qkv_weight, proj_weight, expand_weight, reduce_weight, bias_table):
    tile_rows, tile_cols, channels = tile.shape
    head_count = HEADS
    head_size = channels // head_count
    normed = layer_norm(tile, norm_gain[layer, 0], norm_shift[layer, 0])
    projected = jnp.dot(normed.reshape(-1, channels), qkv_weight[layer], preferred_element_type=jnp.float32).astype(jnp.bfloat16)
    projected = to_windows(projected.reshape(tile_rows, tile_cols, 3, head_count, head_size), tile_rows, tile_cols)
    query = projected[:, :, 0].astype(jnp.float32)
    keys = projected[:, :, 1].astype(jnp.float32)
    values = projected[:, :, 2].astype(jnp.float32)
    bias = bias_table[layer][:, bias_index]
    scores = jnp.einsum('nqhd,nkhd->nhqk', query, keys) * head_size ** (-0.5) + bias
    if region is not None:
        window_region = to_windows(region, tile_rows, tile_cols)
        same_region = window_region[:, :, None] == window_region[:, None, :]
        scores = jnp.where(same_region[:, None], scores, -jnp.inf)
    row_max = lax.optimization_barrier(jnp.max(scores, -1, keepdims=True))
    raw_weights = jnp.exp(scores - row_max)
    weights = (raw_weights / lax.optimization_barrier(jnp.sum(raw_weights, -1, keepdims=True))).astype(jnp.bfloat16)
    mixed = jnp.einsum('nhqk,nkhd->nqhd', weights.astype(jnp.float32), values).astype(jnp.bfloat16)
    mixed = from_windows(mixed.reshape(-1, WIN * WIN, channels), tile_rows, tile_cols)
    attended = tile + jnp.dot(mixed.reshape(-1, channels), proj_weight[layer], preferred_element_type=jnp.float32).reshape(tile_rows, tile_cols, channels)
    normed_two = layer_norm(attended, norm_gain[layer, 1], norm_shift[layer, 1])
    hidden = jax.nn.gelu(jnp.dot(normed_two.reshape(-1, channels), expand_weight[layer], preferred_element_type=jnp.float32), approximate=False).astype(jnp.bfloat16)
    return attended + jnp.dot(hidden, reduce_weight[layer], preferred_element_type=jnp.float32).reshape(tile_rows, tile_cols, channels)

def reference(tokens, region_ids, bias_index, norm_gain, norm_shift, qkv_weight, proj_weight, expand_weight, reduce_weight, bias_table):
    weights_all = (bias_index, norm_gain, norm_shift, qkv_weight, proj_weight, expand_weight, reduce_weight, bias_table)
    strips = tokens.reshape(NH // WIN, WIN, NW, C)
    first = lax.map(lambda strip: swin_block(strip, 0, None, *weights_all), strips).reshape(NH, NW, C)
    rolled = jnp.roll(first, (-SHIFT, -SHIFT), (0, 1))
    pairs = (rolled.reshape(NH // WIN, WIN, NW, C), region_ids.reshape(NH // WIN, WIN, NW))
    second = lax.map(lambda pair: swin_block(pair[0], 1, pair[1], *weights_all), pairs).reshape(NH, NW, C)
    return jnp.roll(second, (SHIFT, SHIFT), (0, 1))
```

```python
import functools
import math

import jax
import jax.numpy as jnp
from jax import lax
from jax.experimental import pallas as pl
from jax.experimental.pallas import tpu as pltpu
from jax.sharding import PartitionSpec as P

HEADS = 8
LOG2E = math.log2(math.e)
ENTRIES = 961
FIXED = 8000.0
F32 = jnp.float32
BF16 = jnp.bfloat16


def take_lanes(x, lanes):
    return jnp.take_along_axis(x, lanes, axis=1, mode="promise_in_bounds")


def fill_lookup(table, lookup_ref):
    table = jnp.concatenate([table, jnp.zeros((HEADS, 1024 - ENTRIES), F32)], 1)
    fixed = jnp.round(table * FIXED).astype(jnp.int32)
    for pair in range(HEADS // 2):
        packed = (fixed[2 * pair : 2 * pair + 1] << 16) + fixed[2 * pair + 1 : 2 * pair + 2]
        for chunk in range(8):
            lookup_ref[pair * 8 + chunk] = jnp.broadcast_to(
                packed[:, chunk * 128 : chunk * 128 + 128], (8, 128)
            )


def look_up_bias(lookup_ref, index_ref, bias_ref, rows=4, same=None):
    scale = LOG2E / FIXED / 65536

    def tile(row):
        for half in range(2):
            lanes = slice(half * 128, half * 128 + 128)
            index = index_ref[pl.ds(row, 8), lanes]
            low = index & 127
            bits = [(index & bit) != 0 for bit in (128, 256, 512)]
            keep = None if same is None else same(row, lanes)
            for pair in range(HEADS // 2):
                found = [take_lanes(lookup_ref[pair * 8 + chunk], low) for chunk in range(8)]
                for bit in bits:
                    found = [
                        jnp.where(bit, found[2 * i + 1], found[2 * i])
                        for i in range(len(found) // 2)
                    ]
                first = found[0].astype(F32) * scale
                second = (found[0] << 16).astype(F32) * scale
                if keep is not None:
                    first = jnp.where(keep, first, -jnp.inf)
                    second = jnp.where(keep, second, -jnp.inf)
                bias_ref[2 * pair, pl.ds(row, 8), lanes] = first
                bias_ref[2 * pair + 1, pl.ds(row, 8), lanes] = second

    def step(i, carry):
        for sub in range(rows):
            tile(pl.multiple_of(i * (8 * rows) + sub * 8, 8))
        return carry

    lax.fori_loop(0, 32 // rows, step, 0)


def layer_norm(x, gain, shift):
    center = x - jnp.mean(x, -1, keepdims=True)
    spread = jnp.mean(center * center, -1, keepdims=True)
    return (center * lax.rsqrt(spread + 1e-05) * gain + shift).astype(BF16)


def attention(x, normed, bias_ref, wqkv, wproj, joined_ref):
    query = jnp.dot(normed, wqkv[:, 0:256], preferred_element_type=F32)
    query = (query * (LOG2E / math.sqrt(32.0))).astype(BF16)
    keys = jnp.dot(normed, wqkv[:, 256:512], preferred_element_type=F32).astype(BF16)
    values = jnp.dot(normed, wqkv[:, 512:768], preferred_element_type=F32).T.astype(BF16)
    ones = jnp.ones((16, 256), BF16)
    head_of_lane = lax.broadcasted_iota(jnp.int32, (1, 128), 1) // 32
    for h in range(HEADS):
        group = slice((h // 4) * 128, (h // 4) * 128 + 128)
        own = jnp.where(head_of_lane == h % 4, 1.0, 0.0).astype(BF16)
        scores = lax.dot_general(
            keys[:, group], query[:, group] * own, (((1,), (1,)), ((), ())), preferred_element_type=F32
        )
        scores = scores + bias_ref[h]
        raw = jnp.exp2(scores - jnp.max(scores, 0, keepdims=True)).astype(BF16)
        left = jnp.concatenate([values[32 * h : 32 * h + 32], ones], 0)
        out = jnp.dot(left, raw, preferred_element_type=F32)
        inverse = 1.0 / out[32:40]
        for j in range(2):
            part = jnp.concatenate(
                [out[16 * j : 16 * j + 8] * inverse, out[16 * j + 8 : 16 * j + 16] * inverse], 0
            )
            joined_ref[32 * h + 16 * j : 32 * h + 16 * j + 16, :] = part.astype(BF16)
    return x + lax.dot_general(
        joined_ref[...], wproj[...], (((0,), (0,)), ((), ())), preferred_element_type=F32
    )


def feed_forward(attended, normed, wexpand, wreduce):
    total = attended
    for j in range(4):
        part = slice(j * 256, j * 256 + 256)
        hidden = jnp.dot(normed, wexpand[:, part], preferred_element_type=F32)
        hidden = (hidden * (0.5 * lax.erf(hidden * math.sqrt(0.5)) + 0.5)).astype(BF16)
        total = total + jnp.dot(hidden, wreduce[part, :], preferred_element_type=F32)
    return total


def write_quadrants(total, outs):
    cells = total.reshape(2, 8, 2, 8, 256)
    for a in range(2):
        for b in range(2):
            outs[2 * a + b][...] = cells[a, :, b]


def first_kernel(
    x_hbm, index_hbm, table_hbm, gain_hbm, shift_hbm, wqkv_hbm, wproj_hbm, wexpand_hbm, wreduce_hbm,
    out00, out01, out10, out11,
    x, index, table, gain, shift, wqkv, wproj, wexpand, wreduce, lookup, index_t, bias, joined, sems,
):
    moves = [
        (index_hbm, index), (table_hbm.at[0], table), (x_hbm, x), (gain_hbm.at[0], gain), (shift_hbm.at[0], shift),
        (wqkv_hbm.at[0], wqkv), (wproj_hbm.at[0], wproj), (wexpand_hbm.at[0], wexpand), (wreduce_hbm.at[0], wreduce),
    ]
    copies = [pltpu.make_async_copy(src, dst, sems.at[i]) for i, (src, dst) in enumerate(moves)]
    for copy in copies:
        copy.start()
    copies[0].wait()
    copies[1].wait()
    index_t[...] = index[...].T
    fill_lookup(table[...], lookup)
    look_up_bias(lookup, index_t, bias)
    for copy in copies[2:7]:
        copy.wait()
    tile = x[...].reshape(256, 256)
    normed = layer_norm(tile, gain[0:1], shift[0:1])
    attended = attention(tile, normed, bias, wqkv, wproj, joined)
    copies[7].wait()
    copies[8].wait()
    normed = layer_norm(attended, gain[1:2], shift[1:2])
    write_quadrants(feed_forward(attended, normed, wexpand, wreduce), (out00, out01, out10, out11))


def bias_kernel(index, table, region, bias, lookup, index_t, row_label, col_label):
    index_t[...] = index[...].T
    fill_lookup(table[1], lookup)
    labels = region[...].astype(F32).astype(BF16)
    tall_at = lax.broadcasted_iota(jnp.int32, (256, 16), 0)
    tall_lane = lax.broadcasted_iota(jnp.int32, (256, 16), 1)
    wide_at = lax.broadcasted_iota(jnp.int32, (16, 256), 1)
    wide_row = lax.broadcasted_iota(jnp.int32, (16, 256), 0)
    pick_row = jnp.where(tall_at // 16 == tall_lane, 1.0, 0.0).astype(BF16)
    pick_col = jnp.where(wide_at % 16 == wide_row, 1.0, 0.0).astype(BF16)
    tall = jnp.dot(pick_row, labels, preferred_element_type=F32)
    tall = jnp.sum(jnp.where(tall_at % 16 == tall_lane, tall, 0.0), 1, keepdims=True)
    wide = jnp.dot(labels, pick_col, preferred_element_type=F32)
    wide = jnp.sum(jnp.where(wide_at // 16 == wide_row, wide, 0.0), 0, keepdims=True)
    col_label[...] = jnp.broadcast_to(tall, (256, 128))
    row_label[...] = jnp.broadcast_to(wide, (8, 256))

    def same(row, lanes):
        return col_label[pl.ds(row, 8), :] == row_label[:, lanes]

    look_up_bias(lookup, index_t, bias, same=same)


def second_kernel(
    in00, in01, in10, in11, bias, gain, shift, wqkv, wproj, wexpand, wreduce,
    out00, out01, out10, out11, joined,
):
    top = jnp.stack([in00[...], in01[...]], 1)
    bottom = jnp.stack([in10[...], in11[...]], 1)
    tile = jnp.concatenate([top, bottom], 0).reshape(256, 256)
    normed = layer_norm(tile, gain[1, 0:1], shift[1, 0:1])
    attended = attention(tile, normed, bias, wqkv.at[1], wproj.at[1], joined)
    normed = layer_norm(attended, gain[1, 1:2], shift[1, 1:2])
    total = feed_forward(attended, normed, wexpand.at[1], wreduce.at[1])
    write_quadrants(total, (out00, out01, out10, out11))


def shifted(x, rows, cols, by_row, by_col):
    if by_row == 0:
        return lax.ppermute(x, "col", [((c + by_col) % cols, c) for c in range(cols)])
    if by_col == 0:
        return lax.ppermute(x, "row", [((r + by_row) % rows, r) for r in range(rows)])
    pairs = [
        ((r + by_row) % rows * cols + (c + by_col) % cols, r * cols + c)
        for r in range(rows)
        for c in range(cols)
    ]
    return lax.ppermute(x, ("row", "col"), pairs)


def per_device(rows, cols, tokens, region, index, gain, shift, wqkv, wproj, wexpand, wreduce, table):
    hbm = pl.BlockSpec(memory_space=pltpu.HBM)
    vmem = pl.BlockSpec(memory_space=pltpu.VMEM)
    quadrant = jax.ShapeDtypeStruct((8, 8, 256), F32)
    q00, q01, q10, q11 = pl.pallas_call(
        first_kernel,
        out_shape=[quadrant] * 4,
        in_specs=[hbm] * 9,
        out_specs=[vmem] * 4,
        scratch_shapes=[
            pltpu.VMEM((16, 16, 256), F32),
            pltpu.VMEM((256, 256), jnp.int32),
            pltpu.VMEM((HEADS, ENTRIES), F32),
            pltpu.VMEM((2, 256), F32),
            pltpu.VMEM((2, 256), F32),
            pltpu.VMEM((256, 768), BF16),
            pltpu.VMEM((256, 256), BF16),
            pltpu.VMEM((256, 1024), BF16),
            pltpu.VMEM((1024, 256), BF16),
            pltpu.VMEM((32, 8, 128), jnp.int32),
            pltpu.VMEM((256, 256), jnp.int32),
            pltpu.VMEM((HEADS, 256, 256), F32),
            pltpu.VMEM((256, 256), BF16),
            pltpu.SemaphoreType.DMA((9,)),
        ],
        compiler_params=pltpu.CompilerParams(vmem_limit_bytes=63 << 20),
        cost_estimate=pl.CostEstimate(flops=10**9, bytes_accessed=3 << 20, transcendentals=0),
    )(tokens, index, table, gain, shift, wqkv, wproj, wexpand, wreduce)
    r01 = shifted(q10, rows, cols, 0, 1)
    r10 = shifted(q01, rows, cols, 1, 0)
    r11 = shifted(q00, rows, cols, 1, 1)
    bias = pl.pallas_call(
        bias_kernel,
        out_shape=jax.ShapeDtypeStruct((HEADS, 256, 256), F32),
        in_specs=[vmem] * 3,
        out_specs=vmem,
        scratch_shapes=[
            pltpu.VMEM((32, 8, 128), jnp.int32),
            pltpu.VMEM((256, 256), jnp.int32),
            pltpu.VMEM((8, 256), F32),
            pltpu.VMEM((256, 128), F32),
        ],
        compiler_params=pltpu.CompilerParams(vmem_limit_bytes=16 << 20),
        cost_estimate=pl.CostEstimate(flops=10**9, bytes_accessed=8 << 20, transcendentals=0),
    )(index, table, region)
    s00, s01, s10, s11 = pl.pallas_call(
        second_kernel,
        out_shape=[quadrant] * 4,
        in_specs=[vmem] * 11,
        out_specs=[vmem] * 4,
        scratch_shapes=[pltpu.VMEM((256, 256), BF16)],
        compiler_params=pltpu.CompilerParams(vmem_limit_bytes=16 << 20),
        cost_estimate=pl.CostEstimate(flops=10**9, bytes_accessed=3 << 20, transcendentals=0),
    )(q11, r01, r10, r11, bias, gain, shift, wqkv, wproj, wexpand, wreduce)
    t10 = shifted(s01, rows, cols, 0, -1)
    t01 = shifted(s10, rows, cols, -1, 0)
    t00 = shifted(s11, rows, cols, -1, -1)
    top = jnp.concatenate([t00, t01], 1)
    bottom = jnp.concatenate([t10, s00], 1)
    return jnp.concatenate([top, bottom], 0)


def solution(mesh):
    in_specs = (P("row", "col", None), P("row", "col"), P(), P(), P(), P(), P(), P(), P(), P())
    body = functools.partial(per_device, mesh.shape["row"], mesh.shape["col"])
    return jax.shard_map(
        body, mesh=mesh, in_specs=in_specs, out_specs=P("row", "col", None), check_vma=False
    )
```

```python
import functools
import math

import jax
import jax.numpy as jnp
from jax import lax
from jax.experimental import pallas as pl
from jax.experimental.pallas import tpu as pltpu
from jax.sharding import PartitionSpec as P

HEADS = 8
LOG2E = math.log2(math.e)
ENTRIES = 961
FIXED = 8000.0
F32 = jnp.float32
BF16 = jnp.bfloat16


def take_lanes(x, lanes):
    return jnp.take_along_axis(x, lanes, axis=1, mode="promise_in_bounds")


def fill_lookup(table, lookup_ref):
    table = jnp.concatenate([table, jnp.zeros((HEADS, 1024 - ENTRIES), F32)], 1)
    fixed = jnp.round(table * FIXED).astype(jnp.int32)
    for pair in range(HEADS // 2):
        packed = (fixed[2 * pair : 2 * pair + 1] << 16) + fixed[2 * pair + 1 : 2 * pair + 2]
        for chunk in range(8):
            lookup_ref[pair * 8 + chunk] = jnp.broadcast_to(
                packed[:, chunk * 128 : chunk * 128 + 128], (8, 128)
            )


def look_up_tile(lookup_ref, index_ref, bias_ref, pair, row, half):
    scale = LOG2E / FIXED / 65536
    lanes = slice(half * 128, half * 128 + 128)
    index = index_ref[pl.ds(row, 8), lanes]
    low = index & 127
    found = [take_lanes(lookup_ref[pair * 8 + chunk], low) for chunk in range(8)]
    for bit in (128, 256, 512):
        odd = (index & bit) != 0
        found = [jnp.where(odd, found[2 * i + 1], found[2 * i]) for i in range(len(found) // 2)]
    bias_ref[2 * pair, pl.ds(row, 8), lanes] = found[0].astype(F32) * scale
    bias_ref[2 * pair + 1, pl.ds(row, 8), lanes] = (found[0] << 16).astype(F32) * scale


def look_up_bias(lookup_ref, index_ref, bias_ref, rows=4):
    def step(i, carry):
        for sub in range(rows):
            row = pl.multiple_of(i * (8 * rows) + sub * 8, 8)
            for half in range(2):
                for pair in range(HEADS // 2):
                    look_up_tile(lookup_ref, index_ref, bias_ref, pair, row, half)
        return carry

    lax.fori_loop(0, 32 // rows, step, 0)


def layer_norm(x, gain, shift):
    center = x - jnp.mean(x, -1, keepdims=True)
    spread = jnp.mean(center * center, -1, keepdims=True)
    return (center * lax.rsqrt(spread + 1e-05) * gain + shift).astype(BF16)


AHEAD = 2
EARLY = 64
EACH = 32


def attend(items, score, finish, beside=None):
    items = list(items)
    scores, raw = {}, {}
    for i in range(len(items) + AHEAD + 1):
        if i < len(items):
            scores[i] = score(items[i])
        if beside is not None:
            beside(i)
        if 0 <= i - AHEAD < len(items):
            now = scores.pop(i - AHEAD)
            raw[i - AHEAD] = jnp.exp2(now - jnp.max(now, 0, keepdims=True)).astype(BF16)
        if i - AHEAD >= 1:
            finish(items[i - AHEAD - 1], raw.pop(i - AHEAD - 1))


def attention(x, normed, bias_ref, wqkv, wproj, joined_ref, beside):
    query = jnp.dot(normed, wqkv[:, 0:256], preferred_element_type=F32)
    query = (query * (LOG2E / math.sqrt(32.0))).astype(BF16)
    keys = jnp.dot(normed, wqkv[:, 256:512], preferred_element_type=F32).astype(BF16)
    values = jnp.dot(normed, wqkv[:, 512:768], preferred_element_type=F32).T.astype(BF16)
    ones = jnp.ones((16, 256), BF16)
    head_of_lane = lax.broadcasted_iota(jnp.int32, (1, 128), 1) // 32

    def score(h):
        group = slice((h // 4) * 128, (h // 4) * 128 + 128)
        own = jnp.where(head_of_lane == h % 4, 1.0, 0.0).astype(BF16)
        scores = lax.dot_general(
            keys[:, group], query[:, group] * own, (((1,), (1,)), ((), ())), preferred_element_type=F32
        )
        return scores + bias_ref[h]

    def finish(h, raw):
        left = jnp.concatenate([values[32 * h : 32 * h + 32], ones], 0)
        out = jnp.dot(left, raw, preferred_element_type=F32)
        inverse = 1.0 / out[32:40]
        for j in range(2):
            part = jnp.concatenate(
                [out[16 * j : 16 * j + 8] * inverse, out[16 * j + 8 : 16 * j + 16] * inverse], 0
            )
            joined_ref[32 * h + 16 * j : 32 * h + 16 * j + 16, :] = part.astype(BF16)

    attend(range(HEADS), score, finish, beside)
    return x + lax.dot_general(
        joined_ref[...], wproj[...], (((0,), (0,)), ((), ())), preferred_element_type=F32
    )


def feed_forward(attended, normed, wexpand, wreduce):
    total = attended
    for j in range(4):
        part = slice(j * 256, j * 256 + 256)
        hidden = jnp.dot(normed, wexpand[:, part], preferred_element_type=F32)
        hidden = (hidden * (0.5 * lax.erf(hidden * math.sqrt(0.5)) + 0.5)).astype(BF16)
        total = total + jnp.dot(hidden, wreduce[part, :], preferred_element_type=F32)
    return total


def cell_order(x):
    return jnp.swapaxes(x.reshape(2, 8, 2, 8, x.shape[-1]), 1, 2).reshape(x.shape)


def from_cell_order(x):
    return jnp.swapaxes(x.reshape(2, 2, 8, 8, x.shape[-1]), 1, 2).reshape(x.shape)


def label_row(region):
    labels = region.astype(F32).astype(BF16)
    lane = lax.broadcasted_iota(jnp.int32, (16, 256), 1)
    row = lax.broadcasted_iota(jnp.int32, (16, 256), 0)
    i = (lane // 128) * 8 + (lane // 8) % 8
    j = (lane // 64) % 2 * 8 + lane % 8
    pick_col = jnp.where(j == row, 1.0, 0.0).astype(BF16)
    wide = jnp.dot(labels, pick_col, preferred_element_type=F32)
    return jnp.sum(jnp.where(i == row, wide, 0.0), 0, keepdims=True)


def first_kernel(
    x_hbm, index_hbm, region_hbm, table_hbm, gain_hbm, shift_hbm, wqkv_hbm, wproj_hbm, wexpand_hbm, wreduce_hbm,
    out, top, bottom,
    x, index, region, table, gain, shift, wqkv, wproj, wexpand, wreduce, lookup, index_t, bias, joined, sems,
):
    moves = [
        (index_hbm, index), (table_hbm.at[0], table), (x_hbm, x), (gain_hbm, gain), (shift_hbm, shift),
        (wqkv_hbm.at[0], wqkv), (wproj_hbm.at[0], wproj), (region_hbm, region), (wexpand_hbm.at[0], wexpand),
        (wreduce_hbm.at[0], wreduce),
    ]
    copies = [pltpu.make_async_copy(src, dst, sems.at[i]) for i, (src, dst) in enumerate(moves)]
    for copy in copies:
        copy.start()
    copies[0].wait()
    copies[1].wait()
    index_t[...] = index[...].T
    fill_lookup(table[...], lookup)

    def look_up(tiles):
        for pair, tile in tiles:
            look_up_tile(lookup, index_t, bias, pair, tile // 2 * 8, tile % 2)

    tiles = [(pair, tile) for pair in range(HEADS // 2) for tile in range(64)]
    look_up(tiles[:EARLY])
    for copy in copies[2:8]:
        copy.wait()
    bottom[128:136, :] = jnp.broadcast_to(label_row(region[...]), (8, 256))
    tile = x[...].reshape(256, 256)
    normed = layer_norm(tile, gain[0, 0:1], shift[0, 0:1])
    attended = attention(
        tile, normed, bias, wqkv, wproj, joined,
        lambda i: look_up(tiles[EARLY + i * EACH : EARLY + i * EACH + EACH]),
    )
    copies[8].wait()
    copies[9].wait()
    normed = layer_norm(attended, gain[0, 1:2], shift[0, 1:2])
    total = feed_forward(attended, normed, wexpand, wreduce)
    out[...] = total
    normed = layer_norm(total, gain[1, 0:1], shift[1, 0:1]).astype(F32)
    top[...] = normed[0:128]
    bottom[0:128, :] = normed[128:256]


def side_of(ref, side):
    return ref[0:128, :].reshape(8, 2, 8, 256)[:, side].reshape(64, 256)


def bias_kernel(index, table, top, bottom, bias, own_west, own_east, lookup, index_t):
    for side, strip in enumerate((own_west, own_east)):
        strip[0:64, :] = side_of(top, side)
        strip[64:128, :] = side_of(bottom, side)
    cells = index[...].reshape(2, 8, 2, 8, 256)
    queries = jnp.concatenate(
        [cells[1 - a, :, 1 - b].reshape(64, 256) for a in range(2) for b in range(2)], 0
    )
    index_t[...] = cell_order(queries.T)
    fill_lookup(table[1], lookup)
    look_up_bias(lookup, index_t, bias)


def join_kernel(north, south, bottom, own_west, own_east, to_west, to_east):
    for side, own, strip in ((0, own_west, to_west), (1, own_east, to_east)):
        strip[0:64, :] = side_of(north, side)
        strip[64:192, :] = own[...]
        strip[192:256, :] = side_of(south, side)
    to_east[256:257, :] = bottom[128:129, :]
    to_east[257:264, :] = north[128:135, :]


def second_kernel(
    x, top, bottom, north, south, west, east, bias, gain, shift, wqkv, wproj, wexpand, wreduce,
    out,
    around, keys, values, mask, joined,
):
    def pieces(ref, rows):
        return ref[0:rows, :].reshape(rows // 16, 2, 8, 256)

    upper = [pieces(north, 128), pieces(top, 128), pieces(bottom, 128), pieces(south, 128)]
    sides = [west[0:256, :], east[0:256, :]]
    for grid_row in range(4):
        for grid_col in range(4):
            if grid_col in (1, 2):
                cell = upper[grid_row][:, grid_col - 1].reshape(64, 256)
            else:
                cell = sides[grid_col // 3][grid_row * 64 : grid_row * 64 + 64]
            window = grid_row // 2 * 2 + grid_col // 2
            place = (grid_row % 2 * 2 + grid_col % 2) * 64
            around[window, place : place + 64, :] = cell.astype(BF16)

    labels = jnp.concatenate(
        [west[257:258, :], north[128:129, :], west[256:257, :], bottom[128:129, :]], 0
    )
    lane_window = lax.broadcasted_iota(jnp.int32, (4, 256), 1) // 64
    window_row = lax.broadcasted_iota(jnp.int32, (4, 256), 0)
    own_window = lane_window == window_row
    key_label = lax.dot_general(
        labels.astype(BF16), jnp.where(own_window, 1.0, 0.0).astype(BF16), (((0,), (0,)), ((), ())),
        preferred_element_type=F32,
    )
    turned = jnp.concatenate(
        [labels[t : t + 1, (3 - t) * 64 : (4 - t) * 64] for t in range(4)], 1
    )
    mask[...] = jnp.where(key_label == turned, 0.0, -jnp.inf)

    wqkv = wqkv.at[1]
    for window in range(4):
        tokens = around[window]
        key = jnp.dot(tokens, wqkv[:, 256:512], preferred_element_type=F32).astype(BF16)
        value = jnp.dot(tokens, wqkv[:, 512:768], preferred_element_type=F32).T.astype(BF16)
        for group in range(2):
            keys[group, window // 2, :, window % 2 * 128 : window % 2 * 128 + 128] = key[
                :, group * 128 : group * 128 + 128
            ]
        for h in range(HEADS):
            values[h, window // 2, window % 2 * 32 : window % 2 * 32 + 32, :] = value[h * 32 : h * 32 + 32]
    own = jnp.concatenate([around[t, (3 - t) * 64 : (4 - t) * 64, :] for t in range(4)], 0)
    query = jnp.dot(own, wqkv[:, 0:256], preferred_element_type=F32)
    query = (query * (LOG2E / math.sqrt(32.0))).astype(BF16)

    row = lax.broadcasted_iota(jnp.int32, (128, 256), 0)
    lane = lax.broadcasted_iota(jnp.int32, (128, 256), 1)
    left_cell = lax.broadcasted_iota(jnp.int32, (8, 128), 1) < 64
    ones = jnp.ones((16, 256), BF16)

    def score(item):
        h, half = item
        pick = jnp.where((row // 64 == lane // 128) & (lane % 128 // 32 == h % 4), 1.0, 0.0).astype(BF16)
        group = h // 4
        lanes = slice(half * 128, half * 128 + 128)
        part = query[lanes, group * 128 : group * 128 + 128]
        scores = lax.dot_general(
            keys[group, half], jnp.concatenate([part, part], 1) * pick, (((1,), (1,)), ((), ())),
            preferred_element_type=F32,
        )
        return scores + (bias[h, :, lanes] + mask[:, lanes])

    def finish(item, raw):
        h, half = item
        lanes = slice(half * 128, half * 128 + 128)
        left = jnp.concatenate([values[h, half], ones], 0)
        sums = jnp.dot(left, raw, preferred_element_type=F32)
        inverse = 1.0 / sums[64:72]
        for j in range(2):
            rows = [
                jnp.where(left_cell, sums[at : at + 8], sums[at + 32 : at + 40]) * inverse
                for at in (16 * j, 16 * j + 8)
            ]
            joined[32 * h + 16 * j : 32 * h + 16 * j + 16, lanes] = jnp.concatenate(rows, 0).astype(BF16)

    attend([(h, half) for h in range(HEADS) for half in range(2)], score, finish)
    attended = cell_order(x[...]) + lax.dot_general(
        joined[...], wproj[1], (((0,), (0,)), ((), ())), preferred_element_type=F32
    )
    normed = layer_norm(attended, gain[1, 1:2], shift[1, 1:2])
    total = feed_forward(attended, normed, wexpand.at[1], wreduce.at[1])
    out[...] = from_cell_order(total).reshape(16, 16, 256)


def shifted(x, axis, size, by):
    return lax.ppermute(x, axis, [((i + by) % size, i) for i in range(size)])


HBM = pl.BlockSpec(memory_space=pltpu.HBM)
VMEM = pl.BlockSpec(memory_space=pltpu.VMEM)


def cost(megabytes):
    return pl.CostEstimate(flops=10**9, bytes_accessed=megabytes << 20, transcendentals=0)


def call_first(*args):
    return pl.pallas_call(
        first_kernel,
        out_shape=[
            jax.ShapeDtypeStruct((256, 256), F32),
            jax.ShapeDtypeStruct((128, 256), F32),
            jax.ShapeDtypeStruct((136, 256), F32),
        ],
        in_specs=[HBM] * 10,
        out_specs=[VMEM] * 3,
        scratch_shapes=[
            pltpu.VMEM((16, 16, 256), F32),
            pltpu.VMEM((256, 256), jnp.int32),
            pltpu.VMEM((16, 16), jnp.int32),
            pltpu.VMEM((HEADS, ENTRIES), F32),
            pltpu.VMEM((2, 2, 256), F32),
            pltpu.VMEM((2, 2, 256), F32),
            pltpu.VMEM((256, 768), BF16),
            pltpu.VMEM((256, 256), BF16),
            pltpu.VMEM((256, 1024), BF16),
            pltpu.VMEM((1024, 256), BF16),
            pltpu.VMEM((32, 8, 128), jnp.int32),
            pltpu.VMEM((256, 256), jnp.int32),
            pltpu.VMEM((HEADS, 256, 256), F32),
            pltpu.VMEM((256, 256), BF16),
            pltpu.SemaphoreType.DMA((10,)),
        ],
        compiler_params=pltpu.CompilerParams(vmem_limit_bytes=40 << 20),
        cost_estimate=cost(3),
    )(*args)


def call_bias(*args):
    return pl.pallas_call(
        bias_kernel,
        out_shape=[
            jax.ShapeDtypeStruct((HEADS, 256, 256), F32),
            jax.ShapeDtypeStruct((128, 256), F32),
            jax.ShapeDtypeStruct((128, 256), F32),
        ],
        in_specs=[VMEM] * 4,
        out_specs=[VMEM] * 3,
        scratch_shapes=[
            pltpu.VMEM((32, 8, 128), jnp.int32),
            pltpu.VMEM((256, 256), jnp.int32),
        ],
        compiler_params=pltpu.CompilerParams(vmem_limit_bytes=16 << 20),
        cost_estimate=cost(8),
    )(*args)


def call_join(*args):
    return pl.pallas_call(
        join_kernel,
        out_shape=[jax.ShapeDtypeStruct((256, 256), F32), jax.ShapeDtypeStruct((264, 256), F32)],
        in_specs=[VMEM] * 5,
        out_specs=[VMEM] * 2,
        compiler_params=pltpu.CompilerParams(vmem_limit_bytes=4 << 20),
        cost_estimate=cost(1),
    )(*args)


def call_second(*args):
    return pl.pallas_call(
        second_kernel,
        out_shape=jax.ShapeDtypeStruct((16, 16, 256), F32),
        in_specs=[VMEM] * 14,
        out_specs=VMEM,
        scratch_shapes=[
            pltpu.VMEM((4, 256, 256), BF16),
            pltpu.VMEM((2, 2, 256, 256), BF16),
            pltpu.VMEM((HEADS, 2, 64, 256), BF16),
            pltpu.VMEM((256, 256), F32),
            pltpu.VMEM((256, 256), BF16),
        ],
        compiler_params=pltpu.CompilerParams(vmem_limit_bytes=16 << 20),
        cost_estimate=cost(3),
    )(*args)


def per_device(rows, cols, tokens, region, index, gain, shift, wqkv, wproj, wexpand, wreduce, table):
    resting = [
        pltpu.with_memory_space_constraint(v, pltpu.HBM)
        for v in (tokens, index, region, table, gain, shift, wqkv, wproj, wexpand, wreduce)
    ]
    first, top, bottom = call_first(*resting)
    north = shifted(bottom, "row", rows, -1)
    south = shifted(top, "row", rows, 1)
    bias, own_west, own_east = call_bias(index, table, top, bottom)
    to_west, to_east = call_join(north, south, bottom, own_west, own_east)
    west = shifted(to_east, "col", cols, -1)
    east = shifted(to_west, "col", cols, 1)
    return call_second(
        first, top, bottom, north, south, west, east, bias, gain, shift, wqkv, wproj, wexpand, wreduce
    )


def solution(mesh):
    in_specs = (P("row", "col", None), P("row", "col"), P(), P(), P(), P(), P(), P(), P(), P())
    body = functools.partial(per_device, mesh.shape["row"], mesh.shape["col"])
    return jax.shard_map(
        body, mesh=mesh, in_specs=in_specs, out_specs=P("row", "col", None), check_vma=False
    )
```

```python
import functools
import math

import jax
import jax.numpy as jnp
from jax import lax
from jax.experimental import pallas as pl
from jax.experimental.pallas import tpu as pltpu
from jax.sharding import PartitionSpec as P

HEADS = 8
LOG2E = math.log2(math.e)
ENTRIES = 961
WORDS = (
    ((0, 11, 21), (1, 11, 10), (2, 10, 0)),
    ((3, 11, 21), (4, 11, 10), (5, 10, 0)),
    ((6, 16, 16), (7, 16, 0)),
)
F32 = jnp.float32
BF16 = jnp.bfloat16


def take_lanes(x, lanes):
    return jnp.take_along_axis(x, lanes, axis=1, mode="promise_in_bounds")


def field_scale(bits):
    return (2 ** (bits - 1) - 1) / 4


def fill_lookup(table, lookup_ref):
    table = jnp.concatenate([table, jnp.zeros((HEADS, 1024 - ENTRIES), F32)], 1)
    for at, word in enumerate(WORDS):
        packed = 0
        for head, bits, low in word:
            fixed = jnp.round(table[head : head + 1] * field_scale(bits)).astype(jnp.int32)
            packed = packed | ((fixed & (2**bits - 1)) << low)
        for chunk in range(8):
            lookup_ref[at * 8 + chunk] = jnp.broadcast_to(
                packed[:, chunk * 128 : chunk * 128 + 128], (8, 128)
            )


def look_up_tile(lookup_ref, index_ref, bias_ref, words, row, half):
    lanes = slice(half * 128, half * 128 + 128)
    index = index_ref[pl.ds(row, 8), lanes]
    low_index = index & 127
    odd = [(index & bit) != 0 for bit in (128, 256, 512)]
    for at in words:
        found = [take_lanes(lookup_ref[at * 8 + chunk], low_index) for chunk in range(8)]
        for bit in odd:
            found = [jnp.where(bit, found[2 * i + 1], found[2 * i]) for i in range(len(found) // 2)]
        for head, bits, low in WORDS[at]:
            field = found[0]
            if low + bits < 32:
                field = field << (32 - low - bits)
            field = field >> (32 - bits)
            bias_ref[head, pl.ds(row, 8), lanes] = field.astype(F32) * (LOG2E / field_scale(bits))


def look_up_bias(lookup_ref, index_ref, bias_ref, rows=32):
    def step(i, carry):
        for sub in range(rows):
            row = pl.multiple_of(i * (8 * rows) + sub * 8, 8)
            for half in range(2):
                look_up_tile(lookup_ref, index_ref, bias_ref, range(len(WORDS)), row, half)
        return carry

    lax.fori_loop(0, 32 // rows, step, 0)


def layer_norm(x, gain, shift):
    center = x - jnp.mean(x, -1, keepdims=True)
    spread = jnp.mean(center * center, -1, keepdims=True)
    return (center * lax.rsqrt(spread + 1e-05) * gain + shift).astype(BF16)


AHEAD = 2
EARLY = 64
EACH = 11


def attend(items, score, finish, beside=lambda step: None):
    items = list(items)
    scores, raw = {}, {}
    for i in range(len(items) + AHEAD + 1):
        if i < len(items):
            scores[i] = score(items[i])
        beside(2 * i)
        if 0 <= i - AHEAD < len(items):
            now = scores.pop(i - AHEAD)
            raw[i - AHEAD] = jnp.exp2(now - jnp.max(now, 0, keepdims=True)).astype(BF16)
        beside(2 * i + 1)
        if i - AHEAD >= 1:
            finish(items[i - AHEAD - 1], raw.pop(i - AHEAD - 1))


def attention(x, normed, bias_ref, wqkv, wproj, joined_ref, beside):
    query = jnp.dot(normed, wqkv[:, 0:256], preferred_element_type=F32)
    query = (query * (LOG2E / math.sqrt(32.0))).astype(BF16)
    keys = jnp.dot(normed, wqkv[:, 256:512], preferred_element_type=F32).astype(BF16)
    values = jnp.dot(normed, wqkv[:, 512:768], preferred_element_type=F32).T.astype(BF16)
    ones = jnp.ones((16, 256), BF16)
    head_of_lane = lax.broadcasted_iota(jnp.int32, (1, 128), 1) // 32

    def score(h):
        group = slice((h // 4) * 128, (h // 4) * 128 + 128)
        own = jnp.where(head_of_lane == h % 4, 1.0, 0.0).astype(BF16)
        scores = lax.dot_general(
            keys[:, group], query[:, group] * own, (((1,), (1,)), ((), ())), preferred_element_type=F32
        )
        return scores + bias_ref[h]

    def finish(h, raw):
        left = jnp.concatenate([values[32 * h : 32 * h + 32], ones], 0)
        out = jnp.dot(left, raw, preferred_element_type=F32)
        inverse = 1.0 / out[32:40]
        for j in range(2):
            part = jnp.concatenate(
                [out[16 * j : 16 * j + 8] * inverse, out[16 * j + 8 : 16 * j + 16] * inverse], 0
            )
            joined_ref[32 * h + 16 * j : 32 * h + 16 * j + 16, :] = part.astype(BF16)

    attend(range(HEADS), score, finish, beside)
    return x + lax.dot_general(
        joined_ref[...], wproj[...], (((0,), (0,)), ((), ())), preferred_element_type=F32
    )


def feed_forward(attended, normed, wexpand, wreduce):
    total = attended
    for j in range(4):
        part = slice(j * 256, j * 256 + 256)
        hidden = jnp.dot(normed, wexpand[:, part], preferred_element_type=F32)
        hidden = (hidden * (0.5 * lax.erf(hidden * math.sqrt(0.5)) + 0.5)).astype(BF16)
        total = total + jnp.dot(hidden, wreduce[part, :], preferred_element_type=F32)
    return total


def cell_order(x):
    return jnp.swapaxes(x.reshape(2, 8, 2, 8, x.shape[-1]), 1, 2).reshape(x.shape)


def from_cell_order(x):
    return jnp.swapaxes(x.reshape(2, 2, 8, 8, x.shape[-1]), 1, 2).reshape(x.shape)


def label_row(region):
    labels = region.astype(F32).astype(BF16)
    lane = lax.broadcasted_iota(jnp.int32, (16, 256), 1)
    row = lax.broadcasted_iota(jnp.int32, (16, 256), 0)
    i = (lane // 128) * 8 + (lane // 8) % 8
    j = (lane // 64) % 2 * 8 + lane % 8
    pick_col = jnp.where(j == row, 1.0, 0.0).astype(BF16)
    wide = jnp.dot(labels, pick_col, preferred_element_type=F32)
    return jnp.sum(jnp.where(i == row, wide, 0.0), 0, keepdims=True)


def first_kernel(
    x_hbm, index_hbm, region_hbm, table_hbm, gain_hbm, shift_hbm, wqkv_hbm, wproj_hbm, wexpand_hbm, wreduce_hbm,
    out, top, bottom,
    x, index, region, table, gain, shift, wqkv, wproj, wexpand, wreduce, lookup, index_t, bias, joined, sems,
):
    moves = [
        (index_hbm, index), (table_hbm.at[0], table), (x_hbm, x), (gain_hbm, gain), (shift_hbm, shift),
        (wqkv_hbm.at[0], wqkv), (wproj_hbm.at[0], wproj), (region_hbm, region), (wexpand_hbm.at[0], wexpand),
        (wreduce_hbm.at[0], wreduce),
    ]
    copies = [pltpu.make_async_copy(src, dst, sems.at[i]) for i, (src, dst) in enumerate(moves)]
    for copy in copies:
        copy.start()
    copies[0].wait()
    copies[1].wait()
    index_t[...] = index[...].T
    fill_lookup(table[...], lookup)

    def look_up(tiles):
        for words, tile in tiles:
            look_up_tile(lookup, index_t, bias, words, tile // 2 * 8, tile % 2)

    tiles = [(words, tile) for words in ((0,), (1, 2)) for tile in range(64)]
    look_up(tiles[:EARLY])
    for copy in copies[2:8]:
        copy.wait()
    bottom[128:136, :] = jnp.broadcast_to(label_row(region[...]), (8, 256))
    tile = x[...].reshape(256, 256)
    normed = layer_norm(tile, gain[0, 0:1], shift[0, 0:1])
    attended = attention(
        tile, normed, bias, wqkv, wproj, joined,
        lambda i: look_up(tiles[EARLY + i * EACH : EARLY + i * EACH + EACH]),
    )
    copies[8].wait()
    copies[9].wait()
    normed = layer_norm(attended, gain[0, 1:2], shift[0, 1:2])
    total = feed_forward(attended, normed, wexpand, wreduce)
    out[...] = total
    normed = layer_norm(total, gain[1, 0:1], shift[1, 0:1]).astype(F32)
    top[...] = normed[0:128]
    bottom[0:128, :] = normed[128:256]


def side_of(ref, side):
    return ref[0:128, :].reshape(8, 2, 8, 256)[:, side].reshape(64, 256)


def bias_kernel(index, table, top, bottom, bias, own_west, own_east, lookup, index_t):
    for side, strip in enumerate((own_west, own_east)):
        strip[0:64, :] = side_of(top, side)
        strip[64:128, :] = side_of(bottom, side)
    cells = index[...].reshape(2, 8, 2, 8, 256)
    queries = jnp.concatenate(
        [cells[1 - a, :, 1 - b].reshape(64, 256) for a in range(2) for b in range(2)], 0
    )
    keys = queries.T.reshape(2, 8, 2, 8, 256)
    columns = [keys[:, :, c].reshape(128, 256) for c in range(2)]
    right = lax.broadcasted_iota(jnp.int32, (128, 256), 1) // 64 % 2 == 1
    index_t[0:128, :] = jnp.where(right, columns[0], columns[1])
    index_t[128:256, :] = jnp.where(right, columns[1], columns[0])
    fill_lookup(table[1], lookup)
    look_up_bias(lookup, index_t, bias)


def join_kernel(north, south, bottom, own_west, own_east, to_west, to_east):
    for side, own, strip in ((0, own_west, to_west), (1, own_east, to_east)):
        strip[0:64, :] = side_of(north, side)
        strip[64:192, :] = own[...]
        strip[192:256, :] = side_of(south, side)
    to_east[256:257, :] = bottom[128:129, :]
    to_east[257:264, :] = north[128:135, :]


def project(around, wqkv, keys, values):
    for window in range(4):
        tokens = around[window]
        key = jnp.dot(tokens, wqkv[:, 256:512], preferred_element_type=F32).astype(BF16)
        value = jnp.dot(tokens, wqkv[:, 512:768], preferred_element_type=F32).T.astype(BF16)
        for group in range(2):
            keys[group, window // 2, :, window % 2 * 128 : window % 2 * 128 + 128] = key[
                :, group * 128 : group * 128 + 128
            ]
        for h in range(HEADS):
            values[h, window // 2, window % 2 * 32 : window % 2 * 32 + 32, :] = value[h * 32 : h * 32 + 32]


def cell_scores(keys, query, h, half):
    row = lax.broadcasted_iota(jnp.int32, (128, 256), 0)
    lane = lax.broadcasted_iota(jnp.int32, (128, 256), 1)
    pick = jnp.where((row // 64 == lane // 128) & (lane % 128 // 32 == h % 4), 1.0, 0.0).astype(BF16)
    group = h // 4
    part = query[half * 128 : half * 128 + 128, group * 128 : group * 128 + 128]
    return lax.dot_general(
        keys[group, half], jnp.concatenate([part, part], 1) * pick, (((1,), (1,)), ((), ())),
        preferred_element_type=F32,
    )


def early_kernel(top, bottom, north, south, bias, wqkv, scores, values, query, around, keys):
    for grid_row, ref in enumerate((north, top, bottom, south)):
        for b in range(2):
            place = grid_row % 2 * 64
            around[grid_row // 2 * 2 + b, place : place + 64, :] = side_of(ref, b).astype(BF16)
    wqkv = wqkv.at[1]
    project(around, wqkv, keys, values)
    own = jnp.concatenate([around[t, (1 - t // 2) * 64 : (2 - t // 2) * 64, :] for t in range(4)], 0)
    scaled = jnp.dot(own, wqkv[:, 0:256], preferred_element_type=F32)
    query[...] = (scaled * (LOG2E / math.sqrt(32.0))).astype(BF16)
    for h in range(HEADS):
        for half in range(2):
            lanes = slice(half * 128, half * 128 + 128)
            scores[h, :, lanes] = cell_scores(keys, query, h, half) + bias[h, 0:128, lanes]


def second_kernel(
    x, bottom, north, west, east, bias, early_scores, early_values, query, gain, shift, wqkv, wproj, wexpand, wreduce,
    out,
    around, keys, values, mask, joined,
):
    for grid_row in range(4):
        for b, ref in enumerate((west, east)):
            place = grid_row % 2 * 64
            cell = ref[grid_row * 64 : grid_row * 64 + 64, :]
            around[grid_row // 2 * 2 + b, place : place + 64, :] = cell.astype(BF16)

    labels = [west[257:258, :], north[128:129, :], west[256:257, :], bottom[128:129, :]]
    order = ((1, 3, 0, 2), (0, 2, 1, 3))
    labels = [
        jnp.concatenate([labels[t][:, c * 64 : c * 64 + 64] for c in order[t % 2]], 1) for t in range(4)
    ]
    lane_window = lax.broadcasted_iota(jnp.int32, (4, 256), 1) // 64
    window_row = lax.broadcasted_iota(jnp.int32, (4, 256), 0)
    own_window = lane_window == window_row
    key_label = lax.dot_general(
        jnp.concatenate(labels, 0).astype(BF16), jnp.where(own_window, 1.0, 0.0).astype(BF16),
        (((0,), (0,)), ((), ())), preferred_element_type=F32,
    )
    query_label = jnp.concatenate(
        [labels[t][:, (1 - t // 2) * 64 : (2 - t // 2) * 64] for t in range(4)], 1
    )
    mask[...] = jnp.where(key_label == query_label, 0.0, -jnp.inf)

    project(around, wqkv.at[1], keys, values)
    left_cell = lax.broadcasted_iota(jnp.int32, (8, 128), 1) < 64
    ones = jnp.ones((16, 256), BF16)

    def score(item):
        h, half = item
        lanes = slice(half * 128, half * 128 + 128)
        late = cell_scores(keys, query, h, half) + bias[h, 128:256, lanes]
        return jnp.concatenate([early_scores[h, :, lanes], late], 0) + mask[:, lanes]

    def finish(item, raw):
        h, half = item
        lanes = slice(half * 128, half * 128 + 128)
        left = jnp.concatenate([jnp.concatenate([early_values[h, half], values[h, half]], 1), ones], 0)
        sums = jnp.dot(left, raw, preferred_element_type=F32)
        inverse = 1.0 / sums[64:72]
        for j in range(2):
            rows = [
                jnp.where(left_cell, sums[at : at + 8], sums[at + 32 : at + 40]) * inverse
                for at in (16 * j, 16 * j + 8)
            ]
            joined[32 * h + 16 * j : 32 * h + 16 * j + 16, lanes] = jnp.concatenate(rows, 0).astype(BF16)

    attend([(h, half) for h in range(HEADS) for half in range(2)], score, finish)
    attended = cell_order(x[...]) + lax.dot_general(
        joined[...], wproj[1], (((0,), (0,)), ((), ())), preferred_element_type=F32
    )
    normed = layer_norm(attended, gain[1, 1:2], shift[1, 1:2])
    total = feed_forward(attended, normed, wexpand.at[1], wreduce.at[1])
    out[...] = from_cell_order(total).reshape(16, 16, 256)


def shifted(x, axis, size, by):
    return lax.ppermute(x, axis, [((i + by) % size, i) for i in range(size)])


HBM = pl.BlockSpec(memory_space=pltpu.HBM)
VMEM = pl.BlockSpec(memory_space=pltpu.VMEM)


def cost(megabytes):
    return pl.CostEstimate(flops=10**9, bytes_accessed=megabytes << 20, transcendentals=0)


def call_first(*args):
    return pl.pallas_call(
        first_kernel,
        out_shape=[
            jax.ShapeDtypeStruct((256, 256), F32),
            jax.ShapeDtypeStruct((128, 256), F32),
            jax.ShapeDtypeStruct((136, 256), F32),
        ],
        in_specs=[HBM] * 10,
        out_specs=[VMEM] * 3,
        scratch_shapes=[
            pltpu.VMEM((16, 16, 256), F32),
            pltpu.VMEM((256, 256), jnp.int32),
            pltpu.VMEM((16, 16), jnp.int32),
            pltpu.VMEM((HEADS, ENTRIES), F32),
            pltpu.VMEM((2, 2, 256), F32),
            pltpu.VMEM((2, 2, 256), F32),
            pltpu.VMEM((256, 768), BF16),
            pltpu.VMEM((256, 256), BF16),
            pltpu.VMEM((256, 1024), BF16),
            pltpu.VMEM((1024, 256), BF16),
            pltpu.VMEM((24, 8, 128), jnp.int32),
            pltpu.VMEM((256, 256), jnp.int32),
            pltpu.VMEM((HEADS, 256, 256), F32),
            pltpu.VMEM((256, 256), BF16),
            pltpu.SemaphoreType.DMA((10,)),
        ],
        compiler_params=pltpu.CompilerParams(vmem_limit_bytes=40 << 20),
        cost_estimate=cost(3),
    )(*args)


def call_bias(*args):
    return pl.pallas_call(
        bias_kernel,
        out_shape=[
            jax.ShapeDtypeStruct((HEADS, 256, 256), F32),
            jax.ShapeDtypeStruct((128, 256), F32),
            jax.ShapeDtypeStruct((128, 256), F32),
        ],
        in_specs=[VMEM] * 4,
        out_specs=[VMEM] * 3,
        scratch_shapes=[
            pltpu.VMEM((24, 8, 128), jnp.int32),
            pltpu.VMEM((256, 256), jnp.int32),
        ],
        compiler_params=pltpu.CompilerParams(vmem_limit_bytes=16 << 20),
        cost_estimate=cost(8),
    )(*args)


def call_join(*args):
    return pl.pallas_call(
        join_kernel,
        out_shape=[jax.ShapeDtypeStruct((256, 256), F32), jax.ShapeDtypeStruct((264, 256), F32)],
        in_specs=[VMEM] * 5,
        out_specs=[VMEM] * 2,
        compiler_params=pltpu.CompilerParams(vmem_limit_bytes=4 << 20),
        cost_estimate=cost(1),
    )(*args)


def call_early(*args):
    return pl.pallas_call(
        early_kernel,
        out_shape=[
            jax.ShapeDtypeStruct((HEADS, 128, 256), F32),
            jax.ShapeDtypeStruct((HEADS, 2, 64, 128), BF16),
            jax.ShapeDtypeStruct((256, 256), BF16),
        ],
        in_specs=[VMEM] * 6,
        out_specs=[VMEM] * 3,
        scratch_shapes=[
            pltpu.VMEM((4, 128, 256), BF16),
            pltpu.VMEM((2, 2, 128, 256), BF16),
        ],
        compiler_params=pltpu.CompilerParams(vmem_limit_bytes=16 << 20),
        cost_estimate=cost(8),
    )(*args)


def call_second(*args):
    return pl.pallas_call(
        second_kernel,
        out_shape=jax.ShapeDtypeStruct((16, 16, 256), F32),
        in_specs=[VMEM] * 15,
        out_specs=VMEM,
        scratch_shapes=[
            pltpu.VMEM((4, 128, 256), BF16),
            pltpu.VMEM((2, 2, 128, 256), BF16),
            pltpu.VMEM((HEADS, 2, 64, 128), BF16),
            pltpu.VMEM((256, 256), F32),
            pltpu.VMEM((256, 256), BF16),
        ],
        compiler_params=pltpu.CompilerParams(vmem_limit_bytes=16 << 20),
        cost_estimate=cost(3),
    )(*args)


def per_device(rows, cols, tokens, region, index, gain, shift, wqkv, wproj, wexpand, wreduce, table):
    resting = [
        pltpu.with_memory_space_constraint(v, pltpu.HBM)
        for v in (tokens, index, region, table, gain, shift, wqkv, wproj, wexpand, wreduce)
    ]
    first, top, bottom = call_first(*resting)
    north = shifted(bottom, "row", rows, -1)
    south = shifted(top, "row", rows, 1)
    bias, own_west, own_east = call_bias(index, table, top, bottom)
    to_west, to_east = call_join(north, south, bottom, own_west, own_east)
    west = shifted(to_east, "col", cols, -1)
    east = shifted(to_west, "col", cols, 1)
    scores, values, query = call_early(top, bottom, north, south, bias, wqkv)
    return call_second(
        first, bottom, north, west, east, bias, scores, values, query,
        gain, shift, wqkv, wproj, wexpand, wreduce,
    )


def solution(mesh):
    in_specs = (P("row", "col", None), P("row", "col"), P(), P(), P(), P(), P(), P(), P(), P())
    body = functools.partial(per_device, mesh.shape["row"], mesh.shape["col"])
    return jax.shard_map(
        body, mesh=mesh, in_specs=in_specs, out_specs=P("row", "col", None), check_vma=False
    )
```

```python
import functools
import math

import jax
import jax.numpy as jnp
from jax import lax
from jax.experimental import pallas as pl
from jax.experimental.pallas import tpu as pltpu
from jax.sharding import PartitionSpec as P

HEADS = 8
LOG2E = math.log2(math.e)
ENTRIES = 961
WORDS = (
    ((0, 11, 21), (1, 11, 10), (2, 10, 0)),
    ((3, 11, 21), (4, 11, 10), (5, 10, 0)),
    ((6, 16, 16), (7, 16, 0)),
)
F32 = jnp.float32
BF16 = jnp.bfloat16


def take_lanes(x, lanes):
    return jnp.take_along_axis(x, lanes, axis=1, mode="promise_in_bounds")


def field_scale(bits):
    return (2 ** (bits - 1) - 1) / 4


def fill_lookup(table, lookup_ref):
    table = jnp.concatenate([table, jnp.zeros((HEADS, 1024 - ENTRIES), F32)], 1)
    for at, word in enumerate(WORDS):
        packed = 0
        for head, bits, low in word:
            fixed = jnp.round(table[head : head + 1] * field_scale(bits)).astype(jnp.int32)
            packed = packed | ((fixed & (2**bits - 1)) << low)
        for chunk in range(8):
            lookup_ref[at * 8 + chunk] = jnp.broadcast_to(
                packed[:, chunk * 128 : chunk * 128 + 128], (8, 128)
            )


def look_up_tile(lookup_ref, index_ref, bias_ref, words, row, half):
    lanes = slice(half * 128, half * 128 + 128)
    index = index_ref[pl.ds(row, 8), lanes]
    low_index = index & 127
    odd = [(index & bit) != 0 for bit in (128, 256, 512)]
    for at in words:
        found = [take_lanes(lookup_ref[at * 8 + chunk], low_index) for chunk in range(8)]
        for bit in odd:
            found = [jnp.where(bit, found[2 * i + 1], found[2 * i]) for i in range(len(found) // 2)]
        for head, bits, low in WORDS[at]:
            field = found[0]
            if low + bits < 32:
                field = field << (32 - low - bits)
            field = field >> (32 - bits)
            bias_ref[head, pl.ds(row, 8), lanes] = field.astype(F32) * (LOG2E / field_scale(bits))


def look_up_bias(lookup_ref, index_ref, bias_ref, rows=32):
    def step(i, carry):
        for sub in range(rows):
            row = pl.multiple_of(i * (8 * rows) + sub * 8, 8)
            for half in range(2):
                look_up_tile(lookup_ref, index_ref, bias_ref, range(len(WORDS)), row, half)
        return carry

    lax.fori_loop(0, 32 // rows, step, 0)


def layer_norm(x, gain, shift):
    center = x - jnp.mean(x, -1, keepdims=True)
    spread = jnp.mean(center * center, -1, keepdims=True)
    return (center * lax.rsqrt(spread + 1e-05) * gain + shift).astype(BF16)


AHEAD = 2
LATE_AHEAD = 3
EARLY = 64
EACH = 6


def attend(items, score, finish, beside=lambda step: None, ahead=AHEAD):
    items = list(items)
    scores, raw = {}, {}
    for i in range(len(items) + ahead + 1):
        if i < len(items):
            scores[i] = score(items[i])
        beside(2 * i)
        if 0 <= i - ahead < len(items):
            now = scores.pop(i - ahead)
            raw[i - ahead] = jnp.exp2(now - jnp.max(now, 0, keepdims=True)).astype(BF16)
        beside(2 * i + 1)
        if i - ahead >= 1:
            finish(items[i - ahead - 1], raw.pop(i - ahead - 1))


def attention(x, normed, bias_ref, wqkv, wproj, joined_ref, beside):
    query = jnp.dot(normed, wqkv[:, 0:256], preferred_element_type=F32)
    query = (query * (LOG2E / math.sqrt(32.0))).astype(BF16)
    keys = jnp.dot(normed, wqkv[:, 256:512], preferred_element_type=F32).astype(BF16)
    values = jnp.dot(normed, wqkv[:, 512:768], preferred_element_type=F32).T.astype(BF16)
    ones = jnp.ones((16, 256), BF16)
    head_of_lane = lax.broadcasted_iota(jnp.int32, (1, 128), 1) // 32

    def score(h):
        group = slice((h // 4) * 128, (h // 4) * 128 + 128)
        own = jnp.where(head_of_lane == h % 4, 1.0, 0.0).astype(BF16)
        scores = lax.dot_general(
            keys[:, group], query[:, group] * own, (((1,), (1,)), ((), ())), preferred_element_type=F32
        )
        return scores + bias_ref[h]

    def finish(h, raw):
        left = jnp.concatenate([values[32 * h : 32 * h + 32], ones], 0)
        out = jnp.dot(left, raw, preferred_element_type=F32)
        inverse = 1.0 / out[32:40]
        for j in range(2):
            part = jnp.concatenate(
                [out[16 * j : 16 * j + 8] * inverse, out[16 * j + 8 : 16 * j + 16] * inverse], 0
            )
            joined_ref[32 * h + 16 * j : 32 * h + 16 * j + 16, :] = part.astype(BF16)

    attend(range(HEADS), score, finish, beside)
    return x + lax.dot_general(
        joined_ref[...], wproj[...], (((0,), (0,)), ((), ())), preferred_element_type=F32
    )


def feed_forward(attended, normed, wexpand, wreduce):
    total = attended
    for j in range(4):
        part = slice(j * 256, j * 256 + 256)
        hidden = jnp.dot(normed, wexpand[:, part], preferred_element_type=F32)
        hidden = (hidden * (0.5 * lax.erf(hidden * math.sqrt(0.5)) + 0.5)).astype(BF16)
        total = total + jnp.dot(hidden, wreduce[part, :], preferred_element_type=F32)
    return total


def cell_order(x):
    return jnp.swapaxes(x.reshape(2, 8, 2, 8, x.shape[-1]), 1, 2).reshape(x.shape)


def from_cell_order(x):
    return jnp.swapaxes(x.reshape(2, 2, 8, 8, x.shape[-1]), 1, 2).reshape(x.shape)


def label_row(region):
    labels = region.astype(F32).astype(BF16)
    lane = lax.broadcasted_iota(jnp.int32, (16, 256), 1)
    row = lax.broadcasted_iota(jnp.int32, (16, 256), 0)
    i = (lane // 128) * 8 + (lane // 8) % 8
    j = (lane // 64) % 2 * 8 + lane % 8
    pick_col = jnp.where(j == row, 1.0, 0.0).astype(BF16)
    wide = jnp.dot(labels, pick_col, preferred_element_type=F32)
    return jnp.sum(jnp.where(i == row, wide, 0.0), 0, keepdims=True)


def first_kernel(
    x_hbm, index_hbm, region_hbm, table_hbm, gain_hbm, shift_hbm, wqkv_hbm, wproj_hbm, wexpand_hbm, wreduce_hbm,
    out, top, bottom,
    x, index, region, table, gain, shift, wqkv, wproj, wexpand, wreduce, lookup, index_t, bias, joined, sems,
):
    moves = [
        (index_hbm, index), (table_hbm.at[0], table), (x_hbm, x), (gain_hbm, gain), (shift_hbm, shift),
        (wqkv_hbm.at[0], wqkv), (wproj_hbm.at[0], wproj), (region_hbm, region), (wexpand_hbm.at[0], wexpand),
        (wreduce_hbm.at[0], wreduce),
    ]
    copies = [pltpu.make_async_copy(src, dst, sems.at[i]) for i, (src, dst) in enumerate(moves)]
    for copy in copies:
        copy.start()
    copies[0].wait()
    copies[1].wait()
    index_t[...] = index[...].T
    fill_lookup(table[...], lookup)

    def look_up(tiles):
        for words, tile in tiles:
            look_up_tile(lookup, index_t, bias, words, tile // 2 * 8, tile % 2)

    tiles = [(words, tile) for words in ((0, 1), (2,)) for tile in range(64)]
    look_up(tiles[:EARLY])
    for copy in copies[2:8]:
        copy.wait()
    bottom[128:136, :] = jnp.broadcast_to(label_row(region[...]), (8, 256))
    tile = x[...].reshape(256, 256)
    normed = layer_norm(tile, gain[0, 0:1], shift[0, 0:1])
    attended = attention(
        tile, normed, bias, wqkv, wproj, joined,
        lambda i: look_up(tiles[EARLY + i * EACH : EARLY + i * EACH + EACH]),
    )
    copies[8].wait()
    copies[9].wait()
    normed = layer_norm(attended, gain[0, 1:2], shift[0, 1:2])
    total = feed_forward(attended, normed, wexpand, wreduce)
    out[...] = total
    normed = layer_norm(total, gain[1, 0:1], shift[1, 0:1]).astype(F32)
    top[...] = normed[0:128]
    bottom[0:128, :] = normed[128:256]


def side_of(ref, side):
    return ref[0:128, :].reshape(8, 2, 8, 256)[:, side].reshape(64, 256)


def bias_kernel(index, table, top, bottom, bias, own_west, own_east, lookup, index_t):
    for side, strip in enumerate((own_west, own_east)):
        strip[0:64, :] = side_of(top, side)
        strip[64:128, :] = side_of(bottom, side)
    cells = index[...].reshape(2, 8, 2, 8, 256)
    queries = jnp.concatenate(
        [cells[1 - a, :, 1 - b].reshape(64, 256) for a in range(2) for b in range(2)], 0
    )
    keys = queries.T.reshape(2, 8, 2, 8, 256)
    columns = [keys[:, :, c].reshape(128, 256) for c in range(2)]
    right = lax.broadcasted_iota(jnp.int32, (128, 256), 1) // 64 % 2 == 1
    index_t[0:128, :] = jnp.where(right, columns[0], columns[1])
    index_t[128:256, :] = jnp.where(right, columns[1], columns[0])
    fill_lookup(table[1], lookup)
    look_up_bias(lookup, index_t, bias)


def join_kernel(north, south, bottom, own_west, own_east, to_west, to_east):
    for side, own, strip in ((0, own_west, to_west), (1, own_east, to_east)):
        strip[0:64, :] = side_of(north, side)
        strip[64:192, :] = own[...]
        strip[192:256, :] = side_of(south, side)
    to_east[256:257, :] = bottom[128:129, :]
    to_east[257:264, :] = north[128:135, :]


def project(around, wqkv, keys, values):
    for window in range(4):
        tokens = around[window]
        key = jnp.dot(tokens, wqkv[:, 256:512], preferred_element_type=F32).astype(BF16)
        value = jnp.dot(tokens, wqkv[:, 512:768], preferred_element_type=F32).T.astype(BF16)
        for group in range(2):
            keys[group, window // 2, :, window % 2 * 128 : window % 2 * 128 + 128] = key[
                :, group * 128 : group * 128 + 128
            ]
        for h in range(HEADS):
            values[h, window // 2, window % 2 * 32 : window % 2 * 32 + 32, :] = value[h * 32 : h * 32 + 32]


def cell_scores(keys, query, pair, half):
    row = lax.broadcasted_iota(jnp.int32, (128, 256), 0)
    lane = lax.broadcasted_iota(jnp.int32, (128, 256), 1)
    group = pair // 2
    part = query[half * 128 : half * 128 + 128, group * 128 : group * 128 + 128]
    part = jnp.concatenate([part, part], 1)
    picks = [
        jnp.where((row // 64 == lane // 128) & (lane % 128 // 32 == h % 4), 1.0, 0.0).astype(BF16)
        for h in (2 * pair, 2 * pair + 1)
    ]
    return lax.dot_general(
        keys[group, half], jnp.concatenate([part * pick for pick in picks], 0), (((1,), (1,)), ((), ())),
        preferred_element_type=F32,
    )


def both(ref, pair, rows, lanes):
    return jnp.concatenate([ref[2 * pair, rows, lanes], ref[2 * pair + 1, rows, lanes]], 1)


def early_kernel(top, bottom, north, south, bias, wqkv, scores, values, query, around, keys):
    for grid_row, ref in enumerate((north, top, bottom, south)):
        for b in range(2):
            place = grid_row % 2 * 64
            around[grid_row // 2 * 2 + b, place : place + 64, :] = side_of(ref, b).astype(BF16)
    wqkv = wqkv.at[1]
    project(around, wqkv, keys, values)
    own = jnp.concatenate([around[t, (1 - t // 2) * 64 : (2 - t // 2) * 64, :] for t in range(4)], 0)
    scaled = jnp.dot(own, wqkv[:, 0:256], preferred_element_type=F32)
    query[...] = (scaled * (LOG2E / math.sqrt(32.0))).astype(BF16)
    for pair in range(HEADS // 2):
        for half in range(2):
            lanes = slice(half * 128, half * 128 + 128)
            found = cell_scores(keys, query, pair, half) + both(bias, pair, slice(0, 128), lanes)
            scores[2 * pair, :, lanes] = found[:, 0:128]
            scores[2 * pair + 1, :, lanes] = found[:, 128:256]


def second_kernel(
    x, bottom, north, west, east, bias, early_scores, early_values, query, gain, shift, wqkv, wproj, wexpand, wreduce,
    out,
    around, keys, values, mask, joined,
):
    for grid_row in range(4):
        for b, ref in enumerate((west, east)):
            place = grid_row % 2 * 64
            cell = ref[grid_row * 64 : grid_row * 64 + 64, :]
            around[grid_row // 2 * 2 + b, place : place + 64, :] = cell.astype(BF16)

    labels = [west[257:258, :], north[128:129, :], west[256:257, :], bottom[128:129, :]]
    order = ((1, 3, 0, 2), (0, 2, 1, 3))
    labels = [
        jnp.concatenate([labels[t][:, c * 64 : c * 64 + 64] for c in order[t % 2]], 1) for t in range(4)
    ]
    lane_window = lax.broadcasted_iota(jnp.int32, (4, 256), 1) // 64
    window_row = lax.broadcasted_iota(jnp.int32, (4, 256), 0)
    own_window = lane_window == window_row
    key_label = lax.dot_general(
        jnp.concatenate(labels, 0).astype(BF16), jnp.where(own_window, 1.0, 0.0).astype(BF16),
        (((0,), (0,)), ((), ())), preferred_element_type=F32,
    )
    query_label = jnp.concatenate(
        [labels[t][:, (1 - t // 2) * 64 : (2 - t // 2) * 64] for t in range(4)], 1
    )
    mask[...] = jnp.where(key_label == query_label, 0.0, -jnp.inf)

    project(around, wqkv.at[1], keys, values)
    left_cell = lax.broadcasted_iota(jnp.int32, (8, 128), 1) < 64
    ones = jnp.ones((16, 256), BF16)

    def score(item):
        pair, half = item
        lanes = slice(half * 128, half * 128 + 128)
        late = cell_scores(keys, query, pair, half) + both(bias, pair, slice(128, 256), lanes)
        found = jnp.concatenate([both(early_scores, pair, slice(0, 128), lanes), late], 0)
        return found + jnp.concatenate([mask[:, lanes]] * 2, 1)

    def finish(item, raw):
        pair, half = item
        lanes = slice(half * 128, half * 128 + 128)
        heads = (2 * pair, 2 * pair + 1)
        left = [jnp.concatenate([early_values[h, half], values[h, half]], 1) for h in heads]
        sums = jnp.dot(jnp.concatenate(left + [ones], 0), raw, preferred_element_type=F32)
        for at, h in enumerate(heads):
            mine = sums[:, at * 128 : at * 128 + 128]
            inverse = 1.0 / mine[128:136]
            rows = [
                jnp.where(left_cell, mine[i : i + 8], mine[i + 32 : i + 40]) * inverse
                for i in range(at * 64, at * 64 + 32, 8)
            ]
            for j in range(2):
                part = jnp.concatenate(rows[2 * j : 2 * j + 2], 0).astype(BF16)
                joined[32 * h + 16 * j : 32 * h + 16 * j + 16, lanes] = part

    attend([(pair, half) for pair in range(HEADS // 2) for half in range(2)], score, finish, ahead=LATE_AHEAD)
    attended = cell_order(x[...]) + lax.dot_general(
        joined[...], wproj[1], (((0,), (0,)), ((), ())), preferred_element_type=F32
    )
    normed = layer_norm(attended, gain[1, 1:2], shift[1, 1:2])
    total = feed_forward(attended, normed, wexpand.at[1], wreduce.at[1])
    out[...] = from_cell_order(total).reshape(16, 16, 256)


def shifted(x, axis, size, by):
    return lax.ppermute(x, axis, [((i + by) % size, i) for i in range(size)])


HBM = pl.BlockSpec(memory_space=pltpu.HBM)
VMEM = pl.BlockSpec(memory_space=pltpu.VMEM)


def cost(megabytes):
    return pl.CostEstimate(flops=10**9, bytes_accessed=megabytes << 20, transcendentals=0)


def call_first(*args):
    return pl.pallas_call(
        first_kernel,
        out_shape=[
            jax.ShapeDtypeStruct((256, 256), F32),
            jax.ShapeDtypeStruct((128, 256), F32),
            jax.ShapeDtypeStruct((136, 256), F32),
        ],
        in_specs=[HBM] * 10,
        out_specs=[VMEM] * 3,
        scratch_shapes=[
            pltpu.VMEM((16, 16, 256), F32),
            pltpu.VMEM((256, 256), jnp.int32),
            pltpu.VMEM((16, 16), jnp.int32),
            pltpu.VMEM((HEADS, ENTRIES), F32),
            pltpu.VMEM((2, 2, 256), F32),
            pltpu.VMEM((2, 2, 256), F32),
            pltpu.VMEM((256, 768), BF16),
            pltpu.VMEM((256, 256), BF16),
            pltpu.VMEM((256, 1024), BF16),
            pltpu.VMEM((1024, 256), BF16),
            pltpu.VMEM((24, 8, 128), jnp.int32),
            pltpu.VMEM((256, 256), jnp.int32),
            pltpu.VMEM((HEADS, 256, 256), F32),
            pltpu.VMEM((256, 256), BF16),
            pltpu.SemaphoreType.DMA((10,)),
        ],
        compiler_params=pltpu.CompilerParams(vmem_limit_bytes=40 << 20),
        cost_estimate=cost(3),
    )(*args)


def call_bias(*args):
    return pl.pallas_call(
        bias_kernel,
        out_shape=[
            jax.ShapeDtypeStruct((HEADS, 256, 256), F32),
            jax.ShapeDtypeStruct((128, 256), F32),
            jax.ShapeDtypeStruct((128, 256), F32),
        ],
        in_specs=[VMEM] * 4,
        out_specs=[VMEM] * 3,
        scratch_shapes=[
            pltpu.VMEM((24, 8, 128), jnp.int32),
            pltpu.VMEM((256, 256), jnp.int32),
        ],
        compiler_params=pltpu.CompilerParams(vmem_limit_bytes=16 << 20),
        cost_estimate=cost(8),
    )(*args)


def call_join(*args):
    return pl.pallas_call(
        join_kernel,
        out_shape=[jax.ShapeDtypeStruct((256, 256), F32), jax.ShapeDtypeStruct((264, 256), F32)],
        in_specs=[VMEM] * 5,
        out_specs=[VMEM] * 2,
        compiler_params=pltpu.CompilerParams(vmem_limit_bytes=4 << 20),
        cost_estimate=cost(1),
    )(*args)


def call_early(*args):
    return pl.pallas_call(
        early_kernel,
        out_shape=[
            jax.ShapeDtypeStruct((HEADS, 128, 256), F32),
            jax.ShapeDtypeStruct((HEADS, 2, 64, 128), BF16),
            jax.ShapeDtypeStruct((256, 256), BF16),
        ],
        in_specs=[VMEM] * 6,
        out_specs=[VMEM] * 3,
        scratch_shapes=[
            pltpu.VMEM((4, 128, 256), BF16),
            pltpu.VMEM((2, 2, 128, 256), BF16),
        ],
        compiler_params=pltpu.CompilerParams(vmem_limit_bytes=16 << 20),
        cost_estimate=cost(8),
    )(*args)


def call_second(*args):
    return pl.pallas_call(
        second_kernel,
        out_shape=jax.ShapeDtypeStruct((16, 16, 256), F32),
        in_specs=[VMEM] * 15,
        out_specs=VMEM,
        scratch_shapes=[
            pltpu.VMEM((4, 128, 256), BF16),
            pltpu.VMEM((2, 2, 128, 256), BF16),
            pltpu.VMEM((HEADS, 2, 64, 128), BF16),
            pltpu.VMEM((256, 256), F32),
            pltpu.VMEM((256, 256), BF16),
        ],
        compiler_params=pltpu.CompilerParams(vmem_limit_bytes=16 << 20),
        cost_estimate=cost(3),
    )(*args)


def per_device(rows, cols, tokens, region, index, gain, shift, wqkv, wproj, wexpand, wreduce, table):
    resting = [
        pltpu.with_memory_space_constraint(v, pltpu.HBM)
        for v in (tokens, index, region, table, gain, shift, wqkv, wproj, wexpand, wreduce)
    ]
    first, top, bottom = call_first(*resting)
    north = shifted(bottom, "row", rows, -1)
    south = shifted(top, "row", rows, 1)
    bias, own_west, own_east = call_bias(index, table, top, bottom)
    to_west, to_east = call_join(north, south, bottom, own_west, own_east)
    west = shifted(to_east, "col", cols, -1)
    east = shifted(to_west, "col", cols, 1)
    scores, values, query = call_early(top, bottom, north, south, bias, wqkv)
    return call_second(
        first, bottom, north, west, east, bias, scores, values, query,
        gain, shift, wqkv, wproj, wexpand, wreduce,
    )


def solution(mesh):
    in_specs = (P("row", "col", None), P("row", "col"), P(), P(), P(), P(), P(), P(), P(), P())
    body = functools.partial(per_device, mesh.shape["row"], mesh.shape["col"])
    return jax.shard_map(
        body, mesh=mesh, in_specs=in_specs, out_specs=P("row", "col", None), check_vma=False
    )
```

```python
import functools
import math

import jax
import jax.numpy as jnp
from jax import lax
from jax.experimental import pallas as pl
from jax.experimental.pallas import tpu as pltpu
from jax.sharding import PartitionSpec as P

HEADS = 8
LOG2E = math.log2(math.e)
ENTRIES = 961
WORDS = (
    ((0, 11, 21), (1, 11, 10), (2, 10, 0)),
    ((3, 11, 21), (4, 11, 10), (5, 10, 0)),
    ((6, 16, 16), (7, 16, 0)),
)
F32 = jnp.float32
BF16 = jnp.bfloat16


def take_lanes(x, lanes):
    return jnp.take_along_axis(x, lanes, axis=1, mode="promise_in_bounds")


def field_scale(bits):
    return (2 ** (bits - 1) - 1) / 4


def fill_lookup(table, lookup_ref):
    table = jnp.concatenate([table, jnp.zeros((HEADS, 1024 - ENTRIES), F32)], 1)
    for at, word in enumerate(WORDS):
        packed = 0
        for head, bits, low in word:
            fixed = jnp.round(table[head : head + 1] * field_scale(bits)).astype(jnp.int32)
            packed = packed | ((fixed & (2**bits - 1)) << low)
        for chunk in range(8):
            lookup_ref[at * 8 + chunk] = jnp.broadcast_to(
                packed[:, chunk * 128 : chunk * 128 + 128], (8, 128)
            )


def look_up_tile(lookup_ref, index_ref, bias_ref, words, row, half):
    lanes = slice(half * 128, half * 128 + 128)
    index = index_ref[pl.ds(row, 8), lanes]
    low_index = index & 127
    odd = [(index & bit) != 0 for bit in (128, 256, 512)]
    for at in words:
        found = [take_lanes(lookup_ref[at * 8 + chunk], low_index) for chunk in range(8)]
        for bit in odd:
            found = [jnp.where(bit, found[2 * i + 1], found[2 * i]) for i in range(len(found) // 2)]
        for head, bits, low in WORDS[at]:
            field = found[0]
            if low + bits < 32:
                field = field << (32 - low - bits)
            field = field >> (32 - bits)
            bias_ref[head, pl.ds(row, 8), lanes] = field.astype(F32) * (LOG2E / field_scale(bits))


def look_up_bias(lookup_ref, index_ref, bias_ref, rows=32):
    def step(i, carry):
        for sub in range(rows):
            row = pl.multiple_of(i * (8 * rows) + sub * 8, 8)
            for half in range(2):
                look_up_tile(lookup_ref, index_ref, bias_ref, range(len(WORDS)), row, half)
        return carry

    lax.fori_loop(0, 32 // rows, step, 0)


def layer_norm(x, gain, shift):
    center = x - jnp.mean(x, -1, keepdims=True)
    spread = jnp.mean(center * center, -1, keepdims=True)
    return (center * lax.rsqrt(spread + 1e-05) * gain + shift).astype(BF16)


AHEAD = 2
LATE_AHEAD = 3
EARLY = 64
EACH = 6


def attend(items, score, finish, beside=lambda step: None, ahead=AHEAD):
    items = list(items)
    scores, raw = {}, {}
    for i in range(len(items) + ahead + 1):
        if i < len(items):
            scores[i] = score(items[i])
        beside(2 * i)
        if 0 <= i - ahead < len(items):
            now = scores.pop(i - ahead)
            raw[i - ahead] = jnp.exp2(now - jnp.max(now, 0, keepdims=True)).astype(BF16)
        beside(2 * i + 1)
        if i - ahead >= 1:
            finish(items[i - ahead - 1], raw.pop(i - ahead - 1))


def attention(x, normed, bias_ref, wqkv, wproj, joined_ref, beside):
    query = jnp.dot(normed, wqkv[:, 0:256], preferred_element_type=F32)
    query = (query * (LOG2E / math.sqrt(32.0))).astype(BF16)
    keys = jnp.dot(normed, wqkv[:, 256:512], preferred_element_type=F32).astype(BF16)
    values = jnp.dot(normed, wqkv[:, 512:768], preferred_element_type=F32).T.astype(BF16)
    ones = jnp.ones((16, 256), BF16)
    head_of_lane = lax.broadcasted_iota(jnp.int32, (1, 128), 1) // 32

    def score(h):
        group = slice((h // 4) * 128, (h // 4) * 128 + 128)
        own = jnp.where(head_of_lane == h % 4, 1.0, 0.0).astype(BF16)
        scores = lax.dot_general(
            keys[:, group], query[:, group] * own, (((1,), (1,)), ((), ())), preferred_element_type=F32
        )
        return scores + bias_ref[h]

    def finish(h, raw):
        left = jnp.concatenate([values[32 * h : 32 * h + 32], ones], 0)
        out = jnp.dot(left, raw, preferred_element_type=F32)
        inverse = 1.0 / out[32:40]
        for j in range(2):
            part = jnp.concatenate(
                [out[16 * j : 16 * j + 8] * inverse, out[16 * j + 8 : 16 * j + 16] * inverse], 0
            )
            joined_ref[32 * h + 16 * j : 32 * h + 16 * j + 16, :] = part.astype(BF16)

    attend(range(HEADS), score, finish, beside)
    return x + lax.dot_general(
        joined_ref[...], wproj[...], (((0,), (0,)), ((), ())), preferred_element_type=F32
    )


def feed_forward(attended, normed, wexpand, wreduce):
    total = attended
    for j in range(4):
        part = slice(j * 256, j * 256 + 256)
        hidden = jnp.dot(normed, wexpand[:, part], preferred_element_type=F32)
        hidden = (hidden * (0.5 * lax.erf(hidden * math.sqrt(0.5)) + 0.5)).astype(BF16)
        if j < 3:
            total = total + jnp.dot(hidden, wreduce[part, :], preferred_element_type=F32)
    for rows in (slice(0, 128), slice(128, 256)):
        yield total[rows] + jnp.dot(hidden[rows], wreduce[part, :], preferred_element_type=F32)


def cell_order(x):
    return jnp.swapaxes(x.reshape(2, 8, 2, 8, x.shape[-1]), 1, 2).reshape(x.shape)


def label_row(region):
    labels = region.astype(F32).astype(BF16)
    lane = lax.broadcasted_iota(jnp.int32, (16, 256), 1)
    row = lax.broadcasted_iota(jnp.int32, (16, 256), 0)
    i = (lane // 128) * 8 + (lane // 8) % 8
    j = (lane // 64) % 2 * 8 + lane % 8
    pick_col = jnp.where(j == row, 1.0, 0.0).astype(BF16)
    wide = jnp.dot(labels, pick_col, preferred_element_type=F32)
    return jnp.sum(jnp.where(i == row, wide, 0.0), 0, keepdims=True)


def first_kernel(
    x_hbm, index_hbm, region_hbm, table_hbm, gain_hbm, shift_hbm, wqkv_hbm, wproj_hbm, wexpand_hbm, wreduce_hbm,
    out, top, bottom,
    x, index, region, table, gain, shift, wqkv, wproj, wexpand, wreduce, lookup, index_t, bias, joined, sems,
):
    moves = [
        (index_hbm, index), (table_hbm.at[0], table), (x_hbm, x), (gain_hbm, gain), (shift_hbm, shift),
        (wqkv_hbm.at[0], wqkv), (wproj_hbm.at[0], wproj), (region_hbm, region), (wexpand_hbm.at[0], wexpand),
        (wreduce_hbm.at[0], wreduce),
    ]
    copies = [pltpu.make_async_copy(src, dst, sems.at[i]) for i, (src, dst) in enumerate(moves)]
    for copy in copies:
        copy.start()
    copies[0].wait()
    copies[1].wait()
    index_t[...] = index[...].T
    fill_lookup(table[...], lookup)

    def look_up(tiles):
        for words, tile in tiles:
            look_up_tile(lookup, index_t, bias, words, tile // 2 * 8, tile % 2)

    tiles = [(words, tile) for words in ((0, 1), (2,)) for tile in range(64)]
    look_up(tiles[:EARLY])
    for copy in copies[2:8]:
        copy.wait()
    bottom[128:136, :] = jnp.broadcast_to(label_row(region[...]), (8, 256))
    tile = x[...].reshape(256, 256)
    normed = layer_norm(tile, gain[0, 0:1], shift[0, 0:1])
    attended = attention(
        tile, normed, bias, wqkv, wproj, joined,
        lambda i: look_up(tiles[EARLY + i * EACH : EARLY + i * EACH + EACH]),
    )
    copies[8].wait()
    copies[9].wait()
    normed = layer_norm(attended, gain[0, 1:2], shift[0, 1:2])
    total = jnp.concatenate(list(feed_forward(attended, normed, wexpand, wreduce)), 0)
    out[...] = total
    normed = layer_norm(total, gain[1, 0:1], shift[1, 0:1]).astype(F32)
    top[...] = normed[0:128]
    bottom[0:128, :] = normed[128:256]


def side_of(ref, side):
    return ref[0:128, :].reshape(8, 2, 8, 256)[:, side].reshape(64, 256)


def bias_kernel(index, table, top, bottom, bias, own_west, own_east, lookup, index_t):
    for side, strip in enumerate((own_west, own_east)):
        strip[0:64, :] = side_of(top, side)
        strip[64:128, :] = side_of(bottom, side)
    cells = index[...].reshape(2, 8, 2, 8, 256)
    queries = jnp.concatenate(
        [cells[1 - a, :, 1 - b].reshape(64, 256) for a in range(2) for b in range(2)], 0
    )
    keys = queries.T.reshape(2, 8, 2, 8, 256)
    columns = [keys[:, :, c].reshape(128, 256) for c in range(2)]
    right = lax.broadcasted_iota(jnp.int32, (128, 256), 1) // 64 % 2 == 1
    index_t[0:128, :] = jnp.where(right, columns[0], columns[1])
    index_t[128:256, :] = jnp.where(right, columns[1], columns[0])
    fill_lookup(table[1], lookup)
    look_up_bias(lookup, index_t, bias)


def join_kernel(north, south, bottom, own_west, own_east, to_west, to_east):
    for side, own, strip in ((0, own_west, to_west), (1, own_east, to_east)):
        strip[0:64, :] = side_of(north, side)
        strip[64:192, :] = own[...]
        strip[192:256, :] = side_of(south, side)
    to_east[256:257, :] = bottom[128:129, :]
    to_east[257:264, :] = north[128:135, :]


def project(around, wqkv, keys, values):
    for window in range(4):
        tokens = around[window]
        key = jnp.dot(tokens, wqkv[:, 256:512], preferred_element_type=F32).astype(BF16)
        value = jnp.dot(tokens, wqkv[:, 512:768], preferred_element_type=F32).T.astype(BF16)
        for group in range(2):
            keys[group, window // 2, :, window % 2 * 128 : window % 2 * 128 + 128] = key[
                :, group * 128 : group * 128 + 128
            ]
        for h in range(HEADS):
            values[h, window // 2, window % 2 * 32 : window % 2 * 32 + 32, :] = value[h * 32 : h * 32 + 32]


def cell_scores(keys, query, pair, half):
    row = lax.broadcasted_iota(jnp.int32, (128, 256), 0)
    lane = lax.broadcasted_iota(jnp.int32, (128, 256), 1)
    group = pair // 2
    part = query[half * 128 : half * 128 + 128, group * 128 : group * 128 + 128]
    part = jnp.concatenate([part, part], 1)
    picks = [
        jnp.where((row // 64 == lane // 128) & (lane % 128 // 32 == h % 4), 1.0, 0.0).astype(BF16)
        for h in (2 * pair, 2 * pair + 1)
    ]
    return lax.dot_general(
        keys[group, half], jnp.concatenate([part * pick for pick in picks], 0), (((1,), (1,)), ((), ())),
        preferred_element_type=F32,
    )


def both(ref, pair, rows, lanes):
    return jnp.concatenate([ref[2 * pair, rows, lanes], ref[2 * pair + 1, rows, lanes]], 1)


def early_kernel(top, bottom, north, south, bias, wqkv, scores, values, query, around, keys):
    for grid_row, ref in enumerate((north, top, bottom, south)):
        for b in range(2):
            place = grid_row % 2 * 64
            around[grid_row // 2 * 2 + b, place : place + 64, :] = side_of(ref, b).astype(BF16)
    wqkv = wqkv.at[1]
    project(around, wqkv, keys, values)
    own = jnp.concatenate([around[t, (1 - t // 2) * 64 : (2 - t // 2) * 64, :] for t in range(4)], 0)
    scaled = jnp.dot(own, wqkv[:, 0:256], preferred_element_type=F32)
    query[...] = (scaled * (LOG2E / math.sqrt(32.0))).astype(BF16)
    for pair in range(HEADS // 2):
        for half in range(2):
            lanes = slice(half * 128, half * 128 + 128)
            found = cell_scores(keys, query, pair, half) + both(bias, pair, slice(0, 128), lanes)
            scores[2 * pair, :, lanes] = found[:, 0:128]
            scores[2 * pair + 1, :, lanes] = found[:, 128:256]


def second_kernel(
    x, bottom, north, west, east, bias, early_scores, early_values, query, gain, shift, wqkv, wproj, wexpand, wreduce,
    out,
    around, keys, values, mask, joined, result, sems,
):
    for grid_row in range(4):
        for b, ref in enumerate((west, east)):
            place = grid_row % 2 * 64
            cell = ref[grid_row * 64 : grid_row * 64 + 64, :]
            around[grid_row // 2 * 2 + b, place : place + 64, :] = cell.astype(BF16)

    labels = [west[257:258, :], north[128:129, :], west[256:257, :], bottom[128:129, :]]
    order = ((1, 3, 0, 2), (0, 2, 1, 3))
    labels = [
        jnp.concatenate([labels[t][:, c * 64 : c * 64 + 64] for c in order[t % 2]], 1) for t in range(4)
    ]
    lane_window = lax.broadcasted_iota(jnp.int32, (4, 256), 1) // 64
    window_row = lax.broadcasted_iota(jnp.int32, (4, 256), 0)
    own_window = lane_window == window_row
    key_label = lax.dot_general(
        jnp.concatenate(labels, 0).astype(BF16), jnp.where(own_window, 1.0, 0.0).astype(BF16),
        (((0,), (0,)), ((), ())), preferred_element_type=F32,
    )
    query_label = jnp.concatenate(
        [labels[t][:, (1 - t // 2) * 64 : (2 - t // 2) * 64] for t in range(4)], 1
    )
    mask[...] = jnp.where(key_label == query_label, 0.0, -jnp.inf)

    project(around, wqkv.at[1], keys, values)
    left_cell = lax.broadcasted_iota(jnp.int32, (8, 128), 1) < 64
    ones = jnp.ones((16, 256), BF16)

    def score(item):
        pair, half = item
        lanes = slice(half * 128, half * 128 + 128)
        late = cell_scores(keys, query, pair, half) + both(bias, pair, slice(128, 256), lanes)
        found = jnp.concatenate([both(early_scores, pair, slice(0, 128), lanes), late], 0)
        return found + jnp.concatenate([mask[:, lanes]] * 2, 1)

    def finish(item, raw):
        pair, half = item
        lanes = slice(half * 128, half * 128 + 128)
        heads = (2 * pair, 2 * pair + 1)
        left = [jnp.concatenate([early_values[h, half], values[h, half]], 1) for h in heads]
        sums = jnp.dot(jnp.concatenate(left + [ones], 0), raw, preferred_element_type=F32)
        for at, h in enumerate(heads):
            mine = sums[:, at * 128 : at * 128 + 128]
            inverse = 1.0 / mine[128:136]
            rows = [
                jnp.where(left_cell, mine[i : i + 8], mine[i + 32 : i + 40]) * inverse
                for i in range(at * 64, at * 64 + 32, 8)
            ]
            for j in range(2):
                part = jnp.concatenate(rows[2 * j : 2 * j + 2], 0).astype(BF16)
                joined[32 * h + 16 * j : 32 * h + 16 * j + 16, lanes] = part

    attend([(pair, half) for pair in range(HEADS // 2) for half in range(2)], score, finish, ahead=LATE_AHEAD)
    attended = cell_order(x[...]) + lax.dot_general(
        joined[...], wproj[1], (((0,), (0,)), ((), ())), preferred_element_type=F32
    )
    normed = layer_norm(attended, gain[1, 1:2], shift[1, 1:2])
    copies = []
    for a, total in enumerate(feed_forward(attended, normed, wexpand.at[1], wreduce.at[1])):
        tile_rows = pl.ds(8 * a, 8)
        result[tile_rows] = jnp.swapaxes(total.reshape(2, 8, 8, 256), 0, 1).reshape(8, 16, 256)
        copies.append(pltpu.make_async_copy(result.at[tile_rows], out.at[tile_rows], sems.at[a]))
        copies[a].start()
    for copy in copies:
        copy.wait()


def shifted(x, axis, size, by):
    return lax.ppermute(x, axis, [((i + by) % size, i) for i in range(size)])


HBM = pl.BlockSpec(memory_space=pltpu.HBM)
VMEM = pl.BlockSpec(memory_space=pltpu.VMEM)


def cost(megabytes):
    return pl.CostEstimate(flops=10**9, bytes_accessed=megabytes << 20, transcendentals=0)


def call_first(*args):
    return pl.pallas_call(
        first_kernel,
        out_shape=[
            jax.ShapeDtypeStruct((256, 256), F32),
            jax.ShapeDtypeStruct((128, 256), F32),
            jax.ShapeDtypeStruct((136, 256), F32),
        ],
        in_specs=[HBM] * 10,
        out_specs=[VMEM] * 3,
        scratch_shapes=[
            pltpu.VMEM((16, 16, 256), F32),
            pltpu.VMEM((256, 256), jnp.int32),
            pltpu.VMEM((16, 16), jnp.int32),
            pltpu.VMEM((HEADS, ENTRIES), F32),
            pltpu.VMEM((2, 2, 256), F32),
            pltpu.VMEM((2, 2, 256), F32),
            pltpu.VMEM((256, 768), BF16),
            pltpu.VMEM((256, 256), BF16),
            pltpu.VMEM((256, 1024), BF16),
            pltpu.VMEM((1024, 256), BF16),
            pltpu.VMEM((24, 8, 128), jnp.int32),
            pltpu.VMEM((256, 256), jnp.int32),
            pltpu.VMEM((HEADS, 256, 256), F32),
            pltpu.VMEM((256, 256), BF16),
            pltpu.SemaphoreType.DMA((10,)),
        ],
        compiler_params=pltpu.CompilerParams(vmem_limit_bytes=40 << 20),
        cost_estimate=cost(3),
    )(*args)


def call_bias(*args):
    return pl.pallas_call(
        bias_kernel,
        out_shape=[
            jax.ShapeDtypeStruct((HEADS, 256, 256), F32),
            jax.ShapeDtypeStruct((128, 256), F32),
            jax.ShapeDtypeStruct((128, 256), F32),
        ],
        in_specs=[VMEM] * 4,
        out_specs=[VMEM] * 3,
        scratch_shapes=[
            pltpu.VMEM((24, 8, 128), jnp.int32),
            pltpu.VMEM((256, 256), jnp.int32),
        ],
        compiler_params=pltpu.CompilerParams(vmem_limit_bytes=16 << 20),
        cost_estimate=cost(8),
    )(*args)


def call_join(*args):
    return pl.pallas_call(
        join_kernel,
        out_shape=[jax.ShapeDtypeStruct((256, 256), F32), jax.ShapeDtypeStruct((264, 256), F32)],
        in_specs=[VMEM] * 5,
        out_specs=[VMEM] * 2,
        compiler_params=pltpu.CompilerParams(vmem_limit_bytes=4 << 20),
        cost_estimate=cost(1),
    )(*args)


def call_early(*args):
    return pl.pallas_call(
        early_kernel,
        out_shape=[
            jax.ShapeDtypeStruct((HEADS, 128, 256), F32),
            jax.ShapeDtypeStruct((HEADS, 2, 64, 128), BF16),
            jax.ShapeDtypeStruct((256, 256), BF16),
        ],
        in_specs=[VMEM] * 6,
        out_specs=[VMEM] * 3,
        scratch_shapes=[
            pltpu.VMEM((4, 128, 256), BF16),
            pltpu.VMEM((2, 2, 128, 256), BF16),
        ],
        compiler_params=pltpu.CompilerParams(vmem_limit_bytes=16 << 20),
        cost_estimate=cost(8),
    )(*args)


def call_second(*args):
    return pl.pallas_call(
        second_kernel,
        out_shape=jax.ShapeDtypeStruct((16, 16, 256), F32),
        in_specs=[VMEM] * 15,
        out_specs=HBM,
        scratch_shapes=[
            pltpu.VMEM((4, 128, 256), BF16),
            pltpu.VMEM((2, 2, 128, 256), BF16),
            pltpu.VMEM((HEADS, 2, 64, 128), BF16),
            pltpu.VMEM((256, 256), F32),
            pltpu.VMEM((256, 256), BF16),
            pltpu.VMEM((16, 16, 256), F32),
            pltpu.SemaphoreType.DMA((2,)),
        ],
        compiler_params=pltpu.CompilerParams(vmem_limit_bytes=16 << 20),
        cost_estimate=cost(3),
    )(*args)


def per_device(rows, cols, tokens, region, index, gain, shift, wqkv, wproj, wexpand, wreduce, table):
    resting = [
        pltpu.with_memory_space_constraint(v, pltpu.HBM)
        for v in (tokens, index, region, table, gain, shift, wqkv, wproj, wexpand, wreduce)
    ]
    first, top, bottom = call_first(*resting)
    north = shifted(bottom, "row", rows, -1)
    south = shifted(top, "row", rows, 1)
    bias, own_west, own_east = call_bias(index, table, top, bottom)
    to_west, to_east = call_join(north, south, bottom, own_west, own_east)
    west = shifted(to_east, "col", cols, -1)
    east = shifted(to_west, "col", cols, 1)
    scores, values, query = call_early(top, bottom, north, south, bias, wqkv)
    return call_second(
        first, bottom, north, west, east, bias, scores, values, query,
        gain, shift, wqkv, wproj, wexpand, wreduce,
    )


def solution(mesh):
    in_specs = (P("row", "col", None), P("row", "col"), P(), P(), P(), P(), P(), P(), P(), P())
    body = functools.partial(per_device, mesh.shape["row"], mesh.shape["col"])
    return jax.shard_map(
        body, mesh=mesh, in_specs=in_specs, out_specs=P("row", "col", None), check_vma=False
    )
```

```python
import functools
import math

import jax
import jax.numpy as jnp
from jax import lax
from jax.experimental import pallas as pl
from jax.experimental.pallas import tpu as pltpu
from jax.sharding import PartitionSpec as P

HEADS = 8
LOG2E = math.log2(math.e)
ENTRIES = 961
WORDS = (
    ((0, 11, 21), (1, 11, 10), (2, 10, 0)),
    ((3, 11, 21), (4, 11, 10), (5, 10, 0)),
    ((6, 16, 16), (7, 16, 0)),
)
F32 = jnp.float32
BF16 = jnp.bfloat16


def take_lanes(x, lanes):
    return jnp.take_along_axis(x, lanes, axis=1, mode="promise_in_bounds")


def field_scale(bits):
    return (2 ** (bits - 1) - 1) / 4


def fill_lookup(table, lookup_ref):
    table = jnp.concatenate([table, jnp.zeros((HEADS, 1024 - ENTRIES), F32)], 1)
    for at, word in enumerate(WORDS):
        packed = 0
        for head, bits, low in word:
            fixed = jnp.round(table[head : head + 1] * field_scale(bits)).astype(jnp.int32)
            packed = packed | ((fixed & (2**bits - 1)) << low)
        for chunk in range(8):
            lookup_ref[at * 8 + chunk] = jnp.broadcast_to(
                packed[:, chunk * 128 : chunk * 128 + 128], (8, 128)
            )


def look_up_tile(lookup_ref, index_ref, bias_ref, words, row, half):
    lanes = slice(half * 128, half * 128 + 128)
    index = index_ref[pl.ds(row, 8), lanes]
    low_index = index & 127
    odd = [(index & bit) != 0 for bit in (128, 256, 512)]
    for at in words:
        found = [take_lanes(lookup_ref[at * 8 + chunk], low_index) for chunk in range(8)]
        for bit in odd:
            found = [jnp.where(bit, found[2 * i + 1], found[2 * i]) for i in range(len(found) // 2)]
        for head, bits, low in WORDS[at]:
            field = found[0]
            if low + bits < 32:
                field = field << (32 - low - bits)
            field = field >> (32 - bits)
            bias_ref[head, pl.ds(row, 8), lanes] = field.astype(F32) * (LOG2E / field_scale(bits))


def look_up_bias(lookup_ref, index_ref, bias_ref, rows=32):
    def step(i, carry):
        for sub in range(rows):
            row = pl.multiple_of(i * (8 * rows) + sub * 8, 8)
            for half in range(2):
                look_up_tile(lookup_ref, index_ref, bias_ref, range(len(WORDS)), row, half)
        return carry

    lax.fori_loop(0, 32 // rows, step, 0)


def layer_norm(x, gain, shift):
    center = x - jnp.mean(x, -1, keepdims=True)
    spread = jnp.mean(center * center, -1, keepdims=True)
    return (center * lax.rsqrt(spread + 1e-05) * gain + shift).astype(BF16)


AHEAD = 2
LATE_AHEAD = 3
EARLY = 64
EACH = 6


def attend(items, score, finish, beside=lambda step: None, ahead=AHEAD):
    items = list(items)
    scores, raw = {}, {}
    for i in range(len(items) + ahead + 1):
        if i < len(items):
            scores[i] = score(items[i])
        beside(2 * i)
        if 0 <= i - ahead < len(items):
            now = scores.pop(i - ahead)
            raw[i - ahead] = jnp.exp2(now - jnp.max(now, 0, keepdims=True)).astype(BF16)
        beside(2 * i + 1)
        if i - ahead >= 1:
            finish(items[i - ahead - 1], raw.pop(i - ahead - 1))


def attention(x, normed, bias_ref, wqkv, wproj, joined_ref, beside):
    query = jnp.dot(normed, wqkv[:, 0:256], preferred_element_type=F32)
    query = (query * (LOG2E / math.sqrt(32.0))).astype(BF16)
    keys = jnp.dot(normed, wqkv[:, 256:512], preferred_element_type=F32).astype(BF16)
    values = jnp.dot(normed, wqkv[:, 512:768], preferred_element_type=F32).T.astype(BF16)
    ones = jnp.ones((16, 256), BF16)
    head_of_lane = lax.broadcasted_iota(jnp.int32, (1, 128), 1) // 32

    def score(h):
        group = slice((h // 4) * 128, (h // 4) * 128 + 128)
        own = jnp.where(head_of_lane == h % 4, 1.0, 0.0).astype(BF16)
        scores = lax.dot_general(
            keys[:, group], query[:, group] * own, (((1,), (1,)), ((), ())), preferred_element_type=F32
        )
        return scores + bias_ref[h]

    def finish(h, raw):
        left = jnp.concatenate([values[32 * h : 32 * h + 32], ones], 0)
        out = jnp.dot(left, raw, preferred_element_type=F32)
        inverse = 1.0 / out[32:40]
        for j in range(2):
            part = jnp.concatenate(
                [out[16 * j : 16 * j + 8] * inverse, out[16 * j + 8 : 16 * j + 16] * inverse], 0
            )
            joined_ref[32 * h + 16 * j : 32 * h + 16 * j + 16, :] = part.astype(BF16)

    attend(range(HEADS), score, finish, beside)
    return x + lax.dot_general(
        joined_ref[...], wproj[...], (((0,), (0,)), ((), ())), preferred_element_type=F32
    )


def feed_forward(attended, normed, wexpand, wreduce):
    total = attended
    for j in range(2):
        part = slice(j * 512, j * 512 + 512)
        hidden = jnp.dot(normed, wexpand[:, part], preferred_element_type=F32)
        hidden = (hidden * (0.5 * lax.erf(hidden * math.sqrt(0.5)) + 0.5)).astype(BF16)
        total = total + jnp.dot(hidden, wreduce[part, :], preferred_element_type=F32)
    return total


def cell_order(x):
    return jnp.swapaxes(x.reshape(2, 8, 2, 8, x.shape[-1]), 1, 2).reshape(x.shape)


def from_cell_order(x):
    return jnp.swapaxes(x.reshape(2, 2, 8, 8, x.shape[-1]), 1, 2).reshape(x.shape)


def label_row(region):
    labels = region.astype(F32).astype(BF16)
    lane = lax.broadcasted_iota(jnp.int32, (16, 256), 1)
    row = lax.broadcasted_iota(jnp.int32, (16, 256), 0)
    i = (lane // 128) * 8 + (lane // 8) % 8
    j = (lane // 64) % 2 * 8 + lane % 8
    pick_col = jnp.where(j == row, 1.0, 0.0).astype(BF16)
    wide = jnp.dot(labels, pick_col, preferred_element_type=F32)
    return jnp.sum(jnp.where(i == row, wide, 0.0), 0, keepdims=True)


def first_kernel(
    x_hbm, index_hbm, region_hbm, table_hbm, gain_hbm, shift_hbm, wqkv_hbm, wproj_hbm, wexpand_hbm, wreduce_hbm,
    out, top, bottom,
    x, index, region, table, gain, shift, wqkv, wproj, wexpand, wreduce, lookup, index_t, bias, joined, sems,
):
    moves = [
        (index_hbm, index), (table_hbm.at[0], table), (x_hbm, x), (gain_hbm, gain), (shift_hbm, shift),
        (wqkv_hbm.at[0], wqkv), (wproj_hbm.at[0], wproj), (region_hbm, region), (wexpand_hbm.at[0], wexpand),
        (wreduce_hbm.at[0], wreduce),
    ]
    copies = [pltpu.make_async_copy(src, dst, sems.at[i]) for i, (src, dst) in enumerate(moves)]
    for copy in copies:
        copy.start()
    copies[0].wait()
    copies[1].wait()
    index_t[...] = index[...].T
    fill_lookup(table[...], lookup)

    def look_up(tiles):
        for words, tile in tiles:
            look_up_tile(lookup, index_t, bias, words, tile // 2 * 8, tile % 2)

    tiles = [(words, tile) for words in ((0, 1), (2,)) for tile in range(64)]
    look_up(tiles[:EARLY])
    for copy in copies[2:8]:
        copy.wait()
    bottom[128:136, :] = jnp.broadcast_to(label_row(region[...]), (8, 256))
    tile = x[...].reshape(256, 256)
    normed = layer_norm(tile, gain[0, 0:1], shift[0, 0:1])
    attended = attention(
        tile, normed, bias, wqkv, wproj, joined,
        lambda i: look_up(tiles[EARLY + i * EACH : EARLY + i * EACH + EACH]),
    )
    copies[8].wait()
    copies[9].wait()
    normed = layer_norm(attended, gain[0, 1:2], shift[0, 1:2])
    total = feed_forward(attended, normed, wexpand, wreduce)
    out[...] = total
    normed = layer_norm(total, gain[1, 0:1], shift[1, 0:1]).astype(F32)
    top[...] = normed[0:128]
    bottom[0:128, :] = normed[128:256]


def side_of(ref, side):
    return ref[0:128, :].reshape(8, 2, 8, 256)[:, side].reshape(64, 256)


def bias_kernel(index, table, top, bottom, bias, own_west, own_east, lookup, index_t):
    for side, strip in enumerate((own_west, own_east)):
        strip[0:64, :] = side_of(top, side)
        strip[64:128, :] = side_of(bottom, side)
    cells = index[...].reshape(2, 8, 2, 8, 256)
    queries = jnp.concatenate(
        [cells[1 - a, :, 1 - b].reshape(64, 256) for a in range(2) for b in range(2)], 0
    )
    keys = queries.T.reshape(2, 8, 2, 8, 256)
    columns = [keys[:, :, c].reshape(128, 256) for c in range(2)]
    right = lax.broadcasted_iota(jnp.int32, (128, 256), 1) // 64 % 2 == 1
    index_t[0:128, :] = jnp.where(right, columns[0], columns[1])
    index_t[128:256, :] = jnp.where(right, columns[1], columns[0])
    fill_lookup(table[1], lookup)
    look_up_bias(lookup, index_t, bias)


def join_kernel(north, south, bottom, own_west, own_east, to_west, to_east):
    for side, own, strip in ((0, own_west, to_west), (1, own_east, to_east)):
        strip[0:64, :] = side_of(north, side)
        strip[64:192, :] = own[...]
        strip[192:256, :] = side_of(south, side)
    to_east[256:257, :] = bottom[128:129, :]
    to_east[257:264, :] = north[128:135, :]


def project(around, wqkv, keys, values):
    for window in range(4):
        tokens = around[window]
        key = jnp.dot(tokens, wqkv[:, 256:512], preferred_element_type=F32).astype(BF16)
        value = jnp.dot(tokens, wqkv[:, 512:768], preferred_element_type=F32).T.astype(BF16)
        for group in range(2):
            keys[group, window // 2, :, window % 2 * 128 : window % 2 * 128 + 128] = key[
                :, group * 128 : group * 128 + 128
            ]
        for h in range(HEADS):
            values[h, window // 2, window % 2 * 32 : window % 2 * 32 + 32, :] = value[h * 32 : h * 32 + 32]


def cell_scores(keys, query, pair, half):
    row = lax.broadcasted_iota(jnp.int32, (128, 256), 0)
    lane = lax.broadcasted_iota(jnp.int32, (128, 256), 1)
    group = pair // 2
    part = query[half * 128 : half * 128 + 128, group * 128 : group * 128 + 128]
    part = jnp.concatenate([part, part], 1)
    picks = [
        jnp.where((row // 64 == lane // 128) & (lane % 128 // 32 == h % 4), 1.0, 0.0).astype(BF16)
        for h in (2 * pair, 2 * pair + 1)
    ]
    return lax.dot_general(
        keys[group, half], jnp.concatenate([part * pick for pick in picks], 0), (((1,), (1,)), ((), ())),
        preferred_element_type=F32,
    )


def both(ref, pair, rows, lanes):
    return jnp.concatenate([ref[2 * pair, rows, lanes], ref[2 * pair + 1, rows, lanes]], 1)


def early_kernel(top, bottom, north, south, bias, wqkv, scores, values, query, around, keys):
    for grid_row, ref in enumerate((north, top, bottom, south)):
        for b in range(2):
            place = grid_row % 2 * 64
            around[grid_row // 2 * 2 + b, place : place + 64, :] = side_of(ref, b).astype(BF16)
    wqkv = wqkv.at[1]
    project(around, wqkv, keys, values)
    own = jnp.concatenate([around[t, (1 - t // 2) * 64 : (2 - t // 2) * 64, :] for t in range(4)], 0)
    scaled = jnp.dot(own, wqkv[:, 0:256], preferred_element_type=F32)
    query[...] = (scaled * (LOG2E / math.sqrt(32.0))).astype(BF16)
    for pair in range(HEADS // 2):
        for half in range(2):
            lanes = slice(half * 128, half * 128 + 128)
            found = cell_scores(keys, query, pair, half) + both(bias, pair, slice(0, 128), lanes)
            scores[2 * pair, :, lanes] = found[:, 0:128]
            scores[2 * pair + 1, :, lanes] = found[:, 128:256]


def second_kernel(
    x, bottom, north, west, east, bias, early_scores, early_values, query, gain, shift, wqkv, wproj, wexpand, wreduce,
    out,
    around, keys, values, mask, joined,
):
    for grid_row in range(4):
        for b, ref in enumerate((west, east)):
            place = grid_row % 2 * 64
            cell = ref[grid_row * 64 : grid_row * 64 + 64, :]
            around[grid_row // 2 * 2 + b, place : place + 64, :] = cell.astype(BF16)

    labels = [west[257:258, :], north[128:129, :], west[256:257, :], bottom[128:129, :]]
    order = ((1, 3, 0, 2), (0, 2, 1, 3))
    labels = [
        jnp.concatenate([labels[t][:, c * 64 : c * 64 + 64] for c in order[t % 2]], 1) for t in range(4)
    ]
    lane_window = lax.broadcasted_iota(jnp.int32, (4, 256), 1) // 64
    window_row = lax.broadcasted_iota(jnp.int32, (4, 256), 0)
    own_window = lane_window == window_row
    key_label = lax.dot_general(
        jnp.concatenate(labels, 0).astype(BF16), jnp.where(own_window, 1.0, 0.0).astype(BF16),
        (((0,), (0,)), ((), ())), preferred_element_type=F32,
    )
    query_label = jnp.concatenate(
        [labels[t][:, (1 - t // 2) * 64 : (2 - t // 2) * 64] for t in range(4)], 1
    )
    mask[...] = jnp.where(key_label == query_label, 0.0, -jnp.inf)

    project(around, wqkv.at[1], keys, values)
    left_cell = lax.broadcasted_iota(jnp.int32, (8, 128), 1) < 64
    ones = jnp.ones((16, 256), BF16)

    def score(item):
        pair, half = item
        lanes = slice(half * 128, half * 128 + 128)
        late = cell_scores(keys, query, pair, half) + both(bias, pair, slice(128, 256), lanes)
        found = jnp.concatenate([both(early_scores, pair, slice(0, 128), lanes), late], 0)
        return found + jnp.concatenate([mask[:, lanes]] * 2, 1)

    def finish(item, raw):
        pair, half = item
        lanes = slice(half * 128, half * 128 + 128)
        heads = (2 * pair, 2 * pair + 1)
        left = [jnp.concatenate([early_values[h, half], values[h, half]], 1) for h in heads]
        sums = jnp.dot(jnp.concatenate(left + [ones], 0), raw, preferred_element_type=F32)
        for at, h in enumerate(heads):
            mine = sums[:, at * 128 : at * 128 + 128]
            inverse = 1.0 / mine[128:136]
            rows = [
                jnp.where(left_cell, mine[i : i + 8], mine[i + 32 : i + 40]) * inverse
                for i in range(at * 64, at * 64 + 32, 8)
            ]
            for j in range(2):
                part = jnp.concatenate(rows[2 * j : 2 * j + 2], 0).astype(BF16)
                joined[32 * h + 16 * j : 32 * h + 16 * j + 16, lanes] = part

    attend([(pair, half) for pair in range(HEADS // 2) for half in range(2)], score, finish, ahead=LATE_AHEAD)
    attended = cell_order(x[...]) + lax.dot_general(
        joined[...], wproj[1], (((0,), (0,)), ((), ())), preferred_element_type=F32
    )
    normed = layer_norm(attended, gain[1, 1:2], shift[1, 1:2])
    total = feed_forward(attended, normed, wexpand.at[1], wreduce.at[1])
    out[...] = from_cell_order(total).reshape(16, 16, 256)


def shifted(x, axis, size, by):
    return lax.ppermute(x, axis, [((i + by) % size, i) for i in range(size)])


HBM = pl.BlockSpec(memory_space=pltpu.HBM)
VMEM = pl.BlockSpec(memory_space=pltpu.VMEM)


def cost(megabytes):
    return pl.CostEstimate(flops=10**9, bytes_accessed=megabytes << 20, transcendentals=0)


def call_first(*args):
    return pl.pallas_call(
        first_kernel,
        out_shape=[
            jax.ShapeDtypeStruct((256, 256), F32),
            jax.ShapeDtypeStruct((128, 256), F32),
            jax.ShapeDtypeStruct((136, 256), F32),
        ],
        in_specs=[HBM] * 10,
        out_specs=[VMEM] * 3,
        scratch_shapes=[
            pltpu.VMEM((16, 16, 256), F32),
            pltpu.VMEM((256, 256), jnp.int32),
            pltpu.VMEM((16, 16), jnp.int32),
            pltpu.VMEM((HEADS, ENTRIES), F32),
            pltpu.VMEM((2, 2, 256), F32),
            pltpu.VMEM((2, 2, 256), F32),
            pltpu.VMEM((256, 768), BF16),
            pltpu.VMEM((256, 256), BF16),
            pltpu.VMEM((256, 1024), BF16),
            pltpu.VMEM((1024, 256), BF16),
            pltpu.VMEM((24, 8, 128), jnp.int32),
            pltpu.VMEM((256, 256), jnp.int32),
            pltpu.VMEM((HEADS, 256, 256), F32),
            pltpu.VMEM((256, 256), BF16),
            pltpu.SemaphoreType.DMA((10,)),
        ],
        compiler_params=pltpu.CompilerParams(vmem_limit_bytes=40 << 20),
        cost_estimate=cost(3),
    )(*args)


def call_bias(*args):
    return pl.pallas_call(
        bias_kernel,
        out_shape=[
            jax.ShapeDtypeStruct((HEADS, 256, 256), F32),
            jax.ShapeDtypeStruct((128, 256), F32),
            jax.ShapeDtypeStruct((128, 256), F32),
        ],
        in_specs=[VMEM] * 4,
        out_specs=[VMEM] * 3,
        scratch_shapes=[
            pltpu.VMEM((24, 8, 128), jnp.int32),
            pltpu.VMEM((256, 256), jnp.int32),
        ],
        compiler_params=pltpu.CompilerParams(vmem_limit_bytes=16 << 20),
        cost_estimate=cost(8),
    )(*args)


def call_join(*args):
    return pl.pallas_call(
        join_kernel,
        out_shape=[jax.ShapeDtypeStruct((256, 256), F32), jax.ShapeDtypeStruct((264, 256), F32)],
        in_specs=[VMEM] * 5,
        out_specs=[VMEM] * 2,
        compiler_params=pltpu.CompilerParams(vmem_limit_bytes=4 << 20),
        cost_estimate=cost(1),
    )(*args)


def call_early(*args):
    return pl.pallas_call(
        early_kernel,
        out_shape=[
            jax.ShapeDtypeStruct((HEADS, 128, 256), F32),
            jax.ShapeDtypeStruct((HEADS, 2, 64, 128), BF16),
            jax.ShapeDtypeStruct((256, 256), BF16),
        ],
        in_specs=[VMEM] * 6,
        out_specs=[VMEM] * 3,
        scratch_shapes=[
            pltpu.VMEM((4, 128, 256), BF16),
            pltpu.VMEM((2, 2, 128, 256), BF16),
        ],
        compiler_params=pltpu.CompilerParams(vmem_limit_bytes=16 << 20),
        cost_estimate=cost(8),
    )(*args)


def call_second(*args):
    return pl.pallas_call(
        second_kernel,
        out_shape=jax.ShapeDtypeStruct((16, 16, 256), F32),
        in_specs=[VMEM] * 15,
        out_specs=VMEM,
        scratch_shapes=[
            pltpu.VMEM((4, 128, 256), BF16),
            pltpu.VMEM((2, 2, 128, 256), BF16),
            pltpu.VMEM((HEADS, 2, 64, 128), BF16),
            pltpu.VMEM((256, 256), F32),
            pltpu.VMEM((256, 256), BF16),
        ],
        compiler_params=pltpu.CompilerParams(vmem_limit_bytes=16 << 20),
        cost_estimate=cost(3),
    )(*args)


def per_device(rows, cols, tokens, region, index, gain, shift, wqkv, wproj, wexpand, wreduce, table):
    resting = [
        pltpu.with_memory_space_constraint(v, pltpu.HBM)
        for v in (tokens, index, region, table, gain, shift, wqkv, wproj, wexpand, wreduce)
    ]
    first, top, bottom = call_first(*resting)
    north = shifted(bottom, "row", rows, -1)
    south = shifted(top, "row", rows, 1)
    bias, own_west, own_east = call_bias(index, table, top, bottom)
    to_west, to_east = call_join(north, south, bottom, own_west, own_east)
    west = shifted(to_east, "col", cols, -1)
    east = shifted(to_west, "col", cols, 1)
    scores, values, query = call_early(top, bottom, north, south, bias, wqkv)
    return call_second(
        first, bottom, north, west, east, bias, scores, values, query,
        gain, shift, wqkv, wproj, wexpand, wreduce,
    )


def solution(mesh):
    in_specs = (P("row", "col", None), P("row", "col"), P(), P(), P(), P(), P(), P(), P(), P())
    body = functools.partial(per_device, mesh.shape["row"], mesh.shape["col"])
    return jax.shard_map(
        body, mesh=mesh, in_specs=in_specs, out_specs=P("row", "col", None), check_vma=False
    )
```
